512 devices in a mesh: seg: 8 (over y), dev: 64 (over z, x, core).
Axes of the slice: x: 4, y: 8, z: 8, core: 2. Of those that a mesh axis runs over, the one named last changes fastest.
Arguments:
- pressure: float32 [1024, 32768], P('seg', 'dev'), may hold values from -6 to 6
- pressure_prev: float32 [1024, 32768], P('seg', 'dev'), may hold values from -6 to 6
- permeability: float32 [1024, 32768], P('seg', 'dev'), may hold values from 0.1 to 2
- u_plus: float32 [4096, 3, 128], P(('seg', 'dev')), may hold values from -6 to 6
- u_minus: bfloat16 [4096, 3, 128], P(('seg', 'dev')), may hold values from -6 to 6
- node_state: int32 [4096, 128], P(('seg', 'dev')), may hold values from 0 to 2
- node_cell: int32 [4096, 128], P(('seg', 'dev')), may hold values from 0 to 65535
- pair_source: int32 [32768], P(('seg', 'dev')), may hold values from 0 to 7
- pair_dest: int32 [32768, 1], P(('seg', 'dev')), may hold values from 0 to 63; in each aligned block of 64 rows (0 to 63, 64 to 127, ...) at most 4 rows name the same one
- pair_target: int32 [32768], P(('seg', 'dev')), may hold values from 0 to 7
- mortar: bfloat16 [32768, 128, 128], P(('seg', 'dev')), may hold values from -0.5 to 0.5
Outputs:
- flow_residual: float32 [1024, 32768], P('seg', 'dev')
- traction_plus: float32 [4096, 3, 128], P(('seg', 'dev'))
- force_minus: float32 [4096, 3, 128], P(('seg', 'dev'))
The draws below stay inside these ranges and needn't reach their ends.
Inputs may be any that keep to these rules, and one draw needn't show every extreme that they name: `pair_dest`: of the 64 pairs held by one device at most 4 name the same destination, and in every draw some device has exactly 4 pairs to one destination.
All inputs are finite; a program needn't handle non-finite values.
Results may differ from the reference program's by a relative error of at most 0.0025.
Values may be sent and summed in bfloat16 or wider, within the bound.
A program may use at most 64 MiB of HBM per device.

```python
import math
import jax
import jax.numpy as jnp
import numpy as np
from jax import lax

NODES = 128
CAP = 4
CS = 128
CD = 512
PATCH_DEV = 8
PAIRS_DEV = 64
NS = 1024
ND = 32768
PATCHES = 4096
PAIRS = 32768
N_SEG = 8
N_DEV = 64


def touch_ends(result, stream_key, low, top_value):
    place = [jax.random.randint(jax.random.fold_in(stream_key, axis), (), 0, length) for axis, length in enumerate(result.shape)]
    main_axis = result.shape.index(max(result.shape))
    next_to = place[:main_axis] + [(place[main_axis] + 1) % result.shape[main_axis]] + place[main_axis + 1:]
    return result.at[tuple(place)].set(low).at[tuple(next_to)].set(top_value)


def steps_of(key, dims, shards, least, top_value):
    loudness = 1.0
    for axis_at, blocks in shards:
        heights = jax.random.uniform(jax.random.fold_in(jax.random.fold_in(key, 6), axis_at), (blocks,), jnp.float32, least / len(shards), top_value / len(shards))
        loudness = loudness * jnp.repeat(jnp.exp(heights), dims[axis_at] // blocks).reshape((-1,) + (1,) * (len(dims) - 1 - axis_at))
    return loudness


def shared_out(rng, own, number, rows, count, top, bound, skew):
    sequence = jax.random.permutation(rng, count)
    heavy_load, usual = shares(count, rows * top, bound, skew, True), shares(count, rows * top, bound, skew, False)
    places = jnp.arange(count)

    def named(tallies, turn):
        used = int((tallies > 0).sum())
        fixed = max(1, used // 4)
        passed = fixed + (places - fixed + turn * (used - fixed)) % max(1, count - fixed)
        return jnp.zeros((count,), jnp.int32).at[sequence[jnp.where(places < fixed, places, passed)]].set(jnp.asarray(tallies, jnp.int32))

    tallies = jnp.where(number % 4 == 0, named(heavy_load, number // 4), named(usual, number - number // 4 - 1))
    mixed = jax.random.permutation(jax.random.fold_in(own, 3), count)
    giver, taker = mixed[0:count // 2 * 2:2], mixed[1:count // 2 * 2:2]
    margin = jnp.minimum(tallies[giver] - 1, bound - tallies[taker]) // 2
    margin = jnp.where((giver == sequence[0]) | (taker == sequence[0]) | (tallies[taker] == 0), 0, jnp.maximum(margin, 0))
    passed = jax.random.randint(jax.random.fold_in(own, 4), (count // 2,), 0, 1 << 20) % (margin + 1)
    tallies = tallies.at[giver].add(-passed).at[taker].add(passed)
    labels = jnp.searchsorted(jnp.cumsum(tallies), jnp.arange(rows * top), side="right").astype(jnp.int32)
    listing = labels.reshape(top, rows).T
    listing = listing[jax.random.permutation(jax.random.fold_in(own, 1), rows)]
    turn = jax.random.randint(jax.random.fold_in(own, 2), (rows, 1), 0, top)
    return jnp.take_along_axis(listing, (jnp.arange(top)[None, :] + turn) % top, axis=1)


def shares(amount, total, bound, skew, full):
    loads = [(1 << 20) // math.isqrt(standing ** skew) + 1 for standing in range(1, amount + 1)]
    largest = bound if full else min(bound, max(-(-total // amount), total * loads[0] // sum(loads)))
    least = 1 if total - largest >= amount - 1 else 0
    holding, rest = [largest] + [least] * (amount - 1), total - largest - least * (amount - 1)
    while rest > 0:
        free = [i for i in range(1, amount) if holding[i] < largest] or [i for i in range(1, amount) if holding[i] < bound]
        whole, budget = sum([loads[i] for i in free]), rest
        for i in free:
            extra = min(bound - holding[i], max(1, budget * loads[i] // whole), rest)
            holding[i] = holding[i] + extra
            rest = rest - extra
    return np.array(holding)


def noise(key, shape, deviation, reach, shards=(), kind=jnp.bfloat16):
    result = jax.random.normal(key, shape, jnp.float32) * deviation
    if len(shards) > 0:
        result = steps_of(key, shape, shards, -0.22, 0.18) * result
    return jnp.clip(result, min=-reach, max=reach).astype(kind)


def setup_inputs(seed: int = 0) -> dict:
    seeds = jax.random.split(jax.random.key(seed), 12)
    pressure = noise(seeds[0], (NS, ND), 1.0, 6.0, ((0, 8), (1, 64)), jnp.float32)
    pressure_prev = noise(seeds[1], (NS, ND), 1.0, 6.0, ((0, 8), (1, 64)), jnp.float32)
    permeability = jnp.clip(jnp.exp(math.log(2.0) - 2.9957323 * jax.random.uniform(seeds[2], (NS, ND), jnp.float32) ** steps_of(seeds[2], (NS, ND), ((0, 8), (1, 64)), -0.2, 0.2)), 0.1, 2.0)
    u_plus = noise(seeds[3], (PATCHES, 3, NODES), 1.0, 6.0, ((0, 512),), jnp.float32)
    u_minus = noise(seeds[4], (PATCHES, 3, NODES), 1.0, 6.0, ((0, 512),))
    node_state = touch_ends(jax.random.randint(seeds[5], (PATCHES, NODES), 0, 3), jax.random.fold_in(seeds[5], 1), 0, 2).astype(jnp.int32)
    node_cell = touch_ends(jax.random.randint(seeds[6], (PATCHES, NODES), 0, CS * CD), jax.random.fold_in(seeds[6], 1), 0, (CS * CD) - 1).astype(jnp.int32)
    pair_source = touch_ends(jax.random.randint(seeds[7], (PAIRS,), 0, PATCH_DEV), jax.random.fold_in(seeds[7], 1), 0, PATCH_DEV - 1).astype(jnp.int32)
    pair_dest_keys = jax.random.split(jax.random.fold_in(seeds[8], 1), PAIRS // PAIRS_DEV)
    pair_dest_turns = jax.random.permutation(jax.random.fold_in(seeds[8], 3), PAIRS // PAIRS_DEV)
    pair_dest = jax.vmap(lambda own, number: shared_out(jax.random.fold_in(seeds[8], 2), own, number, PAIRS_DEV, N_DEV, 1, CAP, 2))(pair_dest_keys, pair_dest_turns).reshape((PAIRS, 1))
    pair_target = touch_ends(jax.random.randint(seeds[9], (PAIRS,), 0, PATCH_DEV), jax.random.fold_in(seeds[9], 1), 0, PATCH_DEV - 1).astype(jnp.int32)
    mortar = noise(seeds[10], (PAIRS, NODES, NODES), NODES ** -0.5, 0.5, ((0, 512),))
    return dict(pressure=pressure, pressure_prev=pressure_prev, permeability=permeability, u_plus=u_plus, u_minus=u_minus, node_state=node_state, node_cell=node_cell, pair_source=pair_source, pair_dest=pair_dest, pair_target=pair_target, mortar=mortar)


COMPRESS = 0.5
PENALTY = 1.5
FRICTION = 0.6
CONFINING = 1.0

def contact_law(jump, node_state, node_pressure):
    normal_part = PENALTY * jump[:, 0]
    tangent = jump[:, 1:]
    stress = CONFINING - node_pressure - normal_part
    limit_stress = FRICTION * jax.nn.softplus(stress)
    factor = limit_stress / jnp.sqrt(lax.optimization_barrier(jnp.sum(tangent * tangent, axis=1)) + 1.0)
    sliding = jnp.concatenate([normal_part[:, None], tangent * factor[:, None]], axis=1)
    state_wide = node_state[:, None, :]
    return jnp.where(state_wide == 0, PENALTY * jump, jnp.where(state_wide == 1, sliding, jnp.zeros_like(jump)))

def cell_residual(padded, pressure, permeability, pressure_prev):
    total = COMPRESS * (pressure - pressure_prev)
    for rows_cut, cols_cut in ((slice(2, None), slice(1, -1)), (slice(0, -2), slice(1, -1)), (slice(1, -1), slice(2, None)), (slice(1, -1), slice(0, -2))):
        neighbor_p = padded[0, rows_cut, cols_cut]
        neighbor_k = padded[1, rows_cut, cols_cut]
        conduct = 2.0 * permeability * neighbor_k / (permeability + neighbor_k)
        total = total + conduct * (pressure - neighbor_p)
    return total

def reference(pressure, pressure_prev, permeability, u_plus, u_minus, node_state, node_cell, pair_source, pair_dest, pair_target, mortar):
    groups = N_SEG * N_DEV
    stacked = jnp.stack([pressure, permeability])
    padded = jnp.pad(stacked, ((0, 0), (1, 1), (1, 1)))
    flow_residual = cell_residual(padded, pressure, permeability, pressure_prev)
    holder = jnp.arange(PAIRS, dtype=jnp.int32) // PAIRS_DEV
    src_global = (holder * PATCH_DEV + pair_source).astype(jnp.int32)
    tgt_global = ((holder // N_DEV * N_DEV + pair_dest[:, 0]) * PATCH_DEV + pair_target).astype(jnp.int32)
    blocks = mortar.reshape(groups, PAIRS_DEV, NODES, NODES)

    def project(block):
        matrices, sources = block
        minus_rows = u_minus[sources].astype(jnp.float32)
        return jnp.einsum('pij,pcj->pci', matrices.astype(jnp.float32), minus_rows, precision=lax.Precision.HIGHEST)
    projected = lax.map(project, (blocks, src_global.reshape(groups, PAIRS_DEV))).reshape(PAIRS, 3, NODES)
    mortar_sum = jax.ops.segment_sum(projected, tgt_global, num_segments=PATCHES)
    jump = u_plus - mortar_sum
    tiles = pressure.reshape(N_SEG, CS, N_DEV, CD).transpose(0, 2, 1, 3).reshape(groups, CS * CD)
    patch_home = (jnp.arange(PATCHES, dtype=jnp.int32) // PATCH_DEV).astype(jnp.int32)
    node_pressure = tiles[patch_home[:, None], node_cell]
    traction_plus = contact_law(jump, node_state, node_pressure)
    traction_half = traction_plus.astype(jnp.bfloat16)
    pair_traction = traction_half[tgt_global]

    def react(block):
        matrices, tractions = block
        return jnp.einsum('pij,pci->pcj', matrices.astype(jnp.float32), tractions.astype(jnp.float32), precision=lax.Precision.HIGHEST)
    reaction = lax.map(react, (blocks, pair_traction.reshape(groups, PAIRS_DEV, 3, NODES))).reshape(PAIRS, 3, NODES)
    force_minus = -jax.ops.segment_sum(reaction, src_global, num_segments=PATCHES)
    return (flow_residual, traction_plus, force_minus)
```

```python
import jax
import jax.numpy as jnp
from jax import lax
from jax.experimental import pallas as pl
from jax.experimental.pallas import tpu as pltpu
from jax.sharding import PartitionSpec as P

CAP = 4
COMPRESS = 0.5
PENALTY = 1.5
FRICTION = 0.6
CONFINING = 1.0

NX = 8
NP = 8
F32 = jnp.float32
BF16 = jnp.bfloat16
I32 = jnp.int32
MESH = pl.DeviceIdType.MESH


def iota(shape, dim):
    return lax.broadcasted_iota(I32, shape, dim)


def split3(value):
    high = value.astype(BF16)
    rest = value - high.astype(F32)
    mid = rest.astype(BF16)
    low = (rest - mid.astype(F32)).astype(BF16)
    return high, mid, low


def dot_nn(a, b):
    return lax.dot_general(a, b, (((1,), (0,)), ((), ())), preferred_element_type=F32)


def dot_nt(a, b):
    return lax.dot_general(a, b, (((1,), (1,)), ((), ())), preferred_element_type=F32)


def dot_tn(a, b):
    return lax.dot_general(a, b, (((0,), (0,)), ((), ())), preferred_element_type=F32)


def remote(src, dst, send, recv, device):
    return pltpu.make_async_remote_copy(
        src_ref=src, dst_ref=dst, send_sem=send, recv_sem=recv, device_id=device, device_id_type=MESH
    )


def exchange_kernel(
    pressure_h, prev_h, perm_h, uplus_r, uminus_r, state_r, cell_r, dest_r, target_r, source_s, mortar_h,
    pair_traction_o, traction_o, flow_o,
    pres, prev, perm, mort, flow, proj, slots_t, owner, zsend, zrecv, csend, crecv, xsend, xrecv,
    tsend, trecv, rsend, rrecv, row_send, row_recv, col_send, col_recv, node_p,
    msem, lsem, zss, zrs, css, crs, xss, xrs, tss, trs, rss, rrs, hss, hrs, osem,
):
    seg = lax.axis_index("seg")
    me = lax.axis_index("dev")
    n_seg = lax.axis_size("seg")
    n_dev = lax.axis_size("dev")
    x = lax.rem(me // 2, NX)
    pos = (me // (2 * NX)) * 2 + lax.rem(me, 2)

    def column(p):
        return {"dev": (p // 2) * (2 * NX) + x * 2 + lax.rem(p, 2)}

    def row(xx):
        return {"dev": (pos // 2) * (2 * NX) + xx * 2 + lax.rem(pos, 2)}

    seg_up, seg_down = {"seg": lax.rem(seg + 1, n_seg)}, {"seg": lax.rem(seg + n_seg - 1, n_seg)}
    dev_up, dev_down = {"dev": lax.rem(me + 1, n_dev)}, {"dev": lax.rem(me + n_dev - 1, n_dev)}

    mcopies = [
        pltpu.make_async_copy(mortar_h.at[pl.ds(8 * g, 8)], mort.at[pl.ds(8 * g, 8)], msem.at[g])
        for g in range(8)
    ]
    for copy in mcopies:
        copy.start()
    lcopies = [
        pltpu.make_async_copy(a, b, lsem.at[i])
        for i, (a, b) in enumerate(((pressure_h, pres), (perm_h, perm), (prev_h, prev)))
    ]
    for copy in lcopies:
        copy.start()

    barrier = pltpu.get_barrier_semaphore()
    for i in range(1, NP):
        pl.semaphore_signal(barrier, inc=1, device_id=column(lax.rem(pos + i, NP)), device_id_type=MESH)
    for i in range(1, NX):
        pl.semaphore_signal(barrier, inc=1, device_id=row(lax.rem(x + i, NX)), device_id_type=MESH)
    for device in (seg_up, seg_down, dev_up, dev_down):
        pl.semaphore_signal(barrier, inc=1, device_id=device, device_id_type=MESH)

    lane, sub = iota((64, 128), 1), iota((64, 128), 0)
    diagonal = lane == sub

    def as_column(ref):
        wide = jnp.concatenate([ref[...].reshape(1, 64), jnp.full((1, 64), -1, I32)], axis=1)
        wide = jnp.broadcast_to(wide, (64, 128))
        return wide, jnp.sum(jnp.where(diagonal, wide, 0), axis=1, keepdims=True)

    dest_row, dest = as_column(dest_r)
    _, target = as_column(target_r)
    rank = jnp.sum(jnp.where((dest_row == dest) & (lane < sub), 1, 0), axis=1, keepdims=True)
    slot = (((dest >> 4) * 2 + (dest & 1)) * NX + ((dest >> 1) & (NX - 1))) * CAP + rank
    for h in range(2):
        slots_t[:, 128 * h : 128 * (h + 1)] = jnp.where(slot == lane + 128 * h, 1.0, 0.0).astype(BF16)
    for p in range(NP):
        code = jnp.sum(jnp.where(slot == (lane & 31) + 32 * p, target, 0), axis=0, keepdims=True)
        csend[p] = jnp.broadcast_to(code.astype(F32), (8, 128))

    for g in range(8):
        mcopies[g].wait()

        def project(j, carry):
            q = 8 * g + j
            value = dot_nt(uminus_r[source_s[q]], mort[q])
            for c in range(3):
                proj[pl.ds(q, 1), 128 * c : 128 * (c + 1)] = value[c : c + 1, :]
            return carry

        lax.fori_loop(0, 8, project, 0, unroll=True)
    parts = split3(proj[...])
    hit = slots_t[...]
    placed = dot_tn(hit, parts[0]) + dot_tn(hit, parts[1]) + dot_tn(hit, parts[2])
    zsend[...] = placed.reshape(NP, 32, 384)

    pl.semaphore_wait(barrier, NP - 1 + NX - 1 + 4)

    zcopies, ccopies = [], []
    for i in range(1, NP):
        p = lax.rem(pos + i, NP)
        ccopies.append(remote(csend.at[p], crecv.at[pos], css.at[i], crs.at[pos], column(p)))
        zcopies.append(remote(zsend.at[p], zrecv.at[pos], zss.at[i], zrs.at[pos], column(p)))
        ccopies[-1].start()
        zcopies[-1].start()
    crecv[pos] = csend[pos]
    zrecv[pos] = zsend[pos]

    for copy in lcopies:
        copy.wait()
    for b in range(4):
        cut = slice(128 * b, 128 * (b + 1))
        row_send[0, b : b + 1, :] = pres[0:1, cut]
        row_send[0, 4 + b : 5 + b, :] = perm[0:1, cut]
        row_send[1, b : b + 1, :] = pres[127:128, cut]
        row_send[1, 4 + b : 5 + b, :] = perm[127:128, cut]
    lane2 = iota((128, 128), 1)
    edge = jnp.where(
        lane2 == 0,
        pres[:, 0:128],
        jnp.where(
            lane2 == 1,
            pltpu.roll(perm[:, 0:128], 1, 1),
            jnp.where(lane2 == 127, pres[:, 384:512], pltpu.roll(perm[:, 384:512], 127, 1)),
        ),
    )
    edge = edge.T
    col_send[0] = edge[0:8, :]
    col_send[1] = edge[120:128, :]
    hcopies = [
        remote(row_send.at[0], row_recv.at[1], hss.at[0], hrs.at[0], seg_down),
        remote(row_send.at[1], row_recv.at[0], hss.at[1], hrs.at[1], seg_up),
        remote(col_send.at[0], col_recv.at[1], hss.at[2], hrs.at[2], dev_down),
        remote(col_send.at[1], col_recv.at[0], hss.at[3], hrs.at[3], dev_up),
    ]
    for copy in hcopies:
        copy.start()

    cell = cell_r[...]
    cell_lane, cell_block = cell & 127, cell >> 7

    def look(r, found):
        lines = pres[pl.ds(pl.multiple_of(8 * r, 8), 8), :]
        for i in range(8):
            for b in range(4):
                line = jnp.broadcast_to(lines[i : i + 1, 128 * b : 128 * (b + 1)], (8, 128))
                picked = jnp.take_along_axis(line, cell_lane, axis=1)
                found = jnp.where(cell_block == 32 * r + (4 * i + b), picked, found)
        return found

    node_p[...] = lax.fori_loop(0, 16, look, jnp.zeros((8, 128), F32))

    for i in range(1, NP):
        p = lax.rem(pos + i, NP)
        remote(csend.at[p], crecv.at[p], css.at[i], crs.at[p], column(p)).wait_recv()
        remote(zsend.at[p], zrecv.at[p], zss.at[i], zrs.at[p], column(p)).wait_recv()
    for h in range(2):
        code = jnp.zeros((8, 128), F32)
        for p in range(4):
            code = jnp.where((iota((8, 128), 1) >> 5) == p, crecv[4 * h + p], code)
        code = jnp.broadcast_to(code[0:1, :], (64, 128)).astype(I32)
        match = (code == (sub & 7)) & (((lane & 31) >> 2) == (sub >> 3))
        owner[:, 128 * h : 128 * (h + 1)] = jnp.where(match, 1.0, 0.0).astype(BF16)
    parts = split3(zrecv[...].reshape(256, 384))
    owners = owner[...]
    dense = dot_nn(owners, parts[0]) + dot_nn(owners, parts[1]) + dot_nn(owners, parts[2])
    xsend[...] = dense.reshape(NX, 8, 384)
    xcopies = []
    for i in range(1, NX):
        xx = lax.rem(x + i, NX)
        xcopies.append(remote(xsend.at[xx], xrecv.at[x], xss.at[i], xrs.at[x], row(xx)))
        xcopies[-1].start()
    xrecv[x] = xsend[x]

    for i in range(4):
        hcopies[i].wait_recv()
    zero_row = jnp.zeros((1, 128), F32)
    above, below = [], []
    for half in range(2):
        for b in range(4):
            above.append(jnp.where(seg > 0, row_recv[0, 4 * half + b : 4 * half + b + 1, :], zero_row))
            below.append(jnp.where(seg < n_seg - 1, row_recv[1, 4 * half + b : 4 * half + b + 1, :], zero_row))
    pres_above, perm_above = jnp.concatenate(above[:4], axis=1), jnp.concatenate(above[4:], axis=1)
    pres_below, perm_below = jnp.concatenate(below[:4], axis=1), jnp.concatenate(below[4:], axis=1)
    sides = jnp.concatenate(
        [
            jnp.where(me > 0, col_recv[0], 0.0),
            jnp.where(me < n_dev - 1, col_recv[1], 0.0),
            jnp.zeros((112, 128), F32),
        ],
        axis=0,
    ).T
    lane8 = iota((8, 512), 1)

    def edge_term(p, k, p2, k2):
        return (2.0 * k * k2 / (k + k2)) * (p - p2)

    for r in range(16):
        rows = slice(8 * r, 8 * (r + 1))
        p, k = pres[rows, :], perm[rows, :]
        if r == 0:
            pu = jnp.concatenate([pres_above, pres[0:7, :]], axis=0)
            ku = jnp.concatenate([perm_above, perm[0:7, :]], axis=0)
        else:
            pu, ku = pres[8 * r - 1 : 8 * r + 7, :], perm[8 * r - 1 : 8 * r + 7, :]
        if r == 15:
            pd = jnp.concatenate([pres[121:128, :], pres_below], axis=0)
            kd = jnp.concatenate([perm[121:128, :], perm_below], axis=0)
        else:
            pd, kd = pres[8 * r + 1 : 8 * r + 9, :], perm[8 * r + 1 : 8 * r + 9, :]
        side = sides[rows, :]
        pl_, kl_ = side[:, 7:8], side[:, 6:7]
        pr_, kr_ = side[:, 8:9], side[:, 9:10]
        pleft = jnp.where(lane8 == 0, pl_, pltpu.roll(p, 1, 1))
        kleft = jnp.where(lane8 == 0, kl_, pltpu.roll(k, 1, 1))
        pright = jnp.where(lane8 == 511, pr_, pltpu.roll(p, 511, 1))
        kright = jnp.where(lane8 == 511, kr_, pltpu.roll(k, 511, 1))
        total = COMPRESS * (p - prev[rows, :])
        total = total + edge_term(p, k, pd, kd) + edge_term(p, k, pu, ku)
        total = total + edge_term(p, k, pright, kright) + edge_term(p, k, pleft, kleft)
        flow[rows, :] = total
    flow_copy = pltpu.make_async_copy(flow, flow_o, osem.at[0])
    flow_copy.start()

    for i in range(1, NX):
        xx = lax.rem(x + i, NX)
        remote(xsend.at[xx], xrecv.at[xx], xss.at[i], xrs.at[xx], row(xx)).wait_recv()
    mortar_sum = xrecv[0]
    for i in range(1, NX):
        mortar_sum = mortar_sum + xrecv[i]
    jump = [uplus_r[:, c, :] - mortar_sum[:, 128 * c : 128 * (c + 1)] for c in range(3)]
    normal_part = PENALTY * jump[0]
    stress = CONFINING - node_p[...] - normal_part
    softplus = jnp.maximum(stress, 0.0) + jnp.log1p(jnp.exp(-jnp.abs(stress)))
    factor = FRICTION * softplus / jnp.sqrt(jump[1] * jump[1] + jump[2] * jump[2] + 1.0)
    state = state_r[...]
    sliding = [normal_part, jump[1] * factor, jump[2] * factor]
    traction = [
        jnp.where(state == 0, PENALTY * jump[c], jnp.where(state == 1, sliding[c], 0.0)) for c in range(3)
    ]
    for c in range(3):
        traction_o[:, 128 * c : 128 * (c + 1)] = traction[c]
    tsend[...] = jnp.concatenate(traction + [jnp.zeros((8, 128), F32)], axis=0).astype(BF16)
    tcopies = []
    for i in range(1, NX):
        xx = lax.rem(x + i, NX)
        tcopies.append(remote(tsend, trecv.at[x], tss.at[i], trs.at[x], row(xx)))
        tcopies[-1].start()
    trecv[x] = tsend[...]
    for i in range(1, NX):
        xx = lax.rem(x + i, NX)
        remote(tsend, trecv.at[xx], tss.at[i], trs.at[xx], row(xx)).wait_recv()

    got = trecv[...].astype(F32)
    table = jnp.concatenate([got[:, 8 * c : 8 * (c + 1), :].reshape(64, 128) for c in range(3)], axis=1)
    rsend[...] = dot_tn(owner[...], table.astype(BF16)).astype(BF16).reshape(NP, 32, 384)
    rcopies = []
    for i in range(1, NP):
        p = lax.rem(pos + i, NP)
        rcopies.append(remote(rsend.at[p], rrecv.at[pos], rss.at[i], rrs.at[pos], column(p)))
        rcopies[-1].start()
    rrecv[pos] = rsend[pos]
    for i in range(1, NP):
        p = lax.rem(pos + i, NP)
        remote(rsend.at[p], rrecv.at[p], rss.at[i], rrs.at[p], column(p)).wait_recv()
    pair_traction_o[...] = dot_nn(slots_t[...], rrecv[...].reshape(256, 384)).astype(BF16)

    for copy in ccopies + zcopies + hcopies + xcopies + tcopies + rcopies:
        copy.wait_send()
    flow_copy.wait()


def reaction_kernel(
    source_s, pair_traction_r, traction_r, flow_h, mortar_h, flow_o, traction_o, force_o, mort, msem, fsem
):
    copies = [
        pltpu.make_async_copy(mortar_h.at[pl.ds(8 * g, 8)], mort.at[pl.ds(8 * g, 8)], msem.at[g])
        for g in range(8)
    ]
    for copy in copies:
        copy.start()
    flow_copy = pltpu.make_async_copy(flow_h, flow_o, fsem)
    flow_copy.start()
    for c in range(3):
        traction_o[:, c, :] = traction_r[:, 128 * c : 128 * (c + 1)]
    patch = iota((8, 128), 0)
    total = jnp.zeros((32, 128), F32)
    for g in range(8):
        copies[g].wait()
        values = pair_traction_r[8 * g : 8 * (g + 1), :].astype(F32)
        for j in range(8):
            q = 8 * g + j
            mine = patch == source_s[q]
            rows = [
                jnp.where(mine, jnp.broadcast_to(values[j : j + 1, 128 * c : 128 * (c + 1)], (8, 128)), 0.0)
                for c in range(3)
            ]
            left = jnp.concatenate(rows + [jnp.zeros((8, 128), F32)], axis=0).astype(BF16)
            total = total + dot_nn(left, mort[q])
    for c in range(3):
        force_o[:, c, :] = -total[8 * c : 8 * (c + 1), :]
    flow_copy.wait()


def on_device(
    pressure, pressure_prev, permeability, u_plus, u_minus, node_state, node_cell,
    pair_source, pair_dest, pair_target, mortar,
):
    any_, vmem, smem = (pl.BlockSpec(memory_space=s) for s in (pl.ANY, pltpu.VMEM, pltpu.SMEM))
    dma = pltpu.SemaphoreType.DMA
    shape = jax.ShapeDtypeStruct
    pair_traction, traction, flow = pl.pallas_call(
        exchange_kernel,
        out_shape=(shape((64, 384), BF16), shape((8, 384), F32), shape((128, 512), F32)),
        in_specs=[any_, any_, any_, vmem, vmem, vmem, vmem, vmem, vmem, smem, any_],
        out_specs=(vmem, vmem, any_),
        scratch_shapes=[
            pltpu.VMEM((128, 512), F32),
            pltpu.VMEM((128, 512), F32),
            pltpu.VMEM((128, 512), F32),
            pltpu.VMEM((64, 128, 128), BF16),
            pltpu.VMEM((128, 512), F32),
            pltpu.VMEM((64, 384), F32),
            pltpu.VMEM((64, 256), BF16),
            pltpu.VMEM((64, 256), BF16),
            pltpu.VMEM((NP, 32, 384), F32),
            pltpu.VMEM((NP, 32, 384), F32),
            pltpu.VMEM((NP, 8, 128), F32),
            pltpu.VMEM((NP, 8, 128), F32),
            pltpu.VMEM((NX, 8, 384), F32),
            pltpu.VMEM((NX, 8, 384), F32),
            pltpu.VMEM((32, 128), BF16),
            pltpu.VMEM((NX, 32, 128), BF16),
            pltpu.VMEM((NP, 32, 384), BF16),
            pltpu.VMEM((NP, 32, 384), BF16),
            pltpu.VMEM((2, 8, 128), F32),
            pltpu.VMEM((2, 8, 128), F32),
            pltpu.VMEM((2, 8, 128), F32),
            pltpu.VMEM((2, 8, 128), F32),
            pltpu.VMEM((8, 128), F32),
            dma((8,)), dma((3,)),
            dma((8,)), dma((8,)), dma((8,)), dma((8,)), dma((8,)), dma((8,)),
            dma((8,)), dma((8,)), dma((8,)), dma((8,)), dma((4,)), dma((4,)), dma((1,)),
        ],
        compiler_params=pltpu.CompilerParams(
            collective_id=0, has_side_effects=True, vmem_limit_bytes=32 * 1024 * 1024
        ),
        name="exchange",
    )(
        pressure, pressure_prev, permeability, u_plus, u_minus, node_state, node_cell,
        pair_dest.reshape(64), pair_target, pair_source, mortar,
    )
    return pl.pallas_call(
        reaction_kernel,
        out_shape=(shape((128, 512), F32), shape((8, 3, 128), F32), shape((8, 3, 128), F32)),
        in_specs=[smem, vmem, vmem, any_, any_],
        out_specs=(any_, vmem, vmem),
        scratch_shapes=[pltpu.VMEM((64, 128, 128), BF16), dma((8,)), dma],
        compiler_params=pltpu.CompilerParams(vmem_limit_bytes=32 * 1024 * 1024),
        name="reaction",
    )(pair_source, pair_traction, traction, flow, mortar)


def solution(mesh):
    both = ("seg", "dev")
    cells, patches = P("seg", "dev"), P(both, None, None)
    placed = (
        cells, cells, cells, patches, patches, P(both, None), P(both, None), P(both), P(both, None), P(both), patches,
    )
    return jax.shard_map(
        on_device, mesh=mesh, in_specs=placed, out_specs=(cells, patches, patches), check_vma=False
    )
```

```python
import jax
import jax.numpy as jnp
from jax import lax
from jax.experimental import pallas as pl
from jax.experimental.pallas import tpu as pltpu
from jax.sharding import PartitionSpec as P

CAP = 4
COMPRESS = 0.5
PENALTY = 1.5
FRICTION = 0.6
CONFINING = 1.0

NP = 8
NZ = 8
F32 = jnp.float32
BF16 = jnp.bfloat16
I32 = jnp.int32
I16 = jnp.int16
MESH = pl.DeviceIdType.MESH


def iota(shape, dim):
    return lax.broadcasted_iota(I32, shape, dim)


def split2(value):
    high = value.astype(BF16)
    return high, (value - high.astype(F32)).astype(BF16)


def dot_nn(a, b):
    return lax.dot_general(a, b, (((1,), (0,)), ((), ())), preferred_element_type=F32)


def dot_nt(a, b):
    return lax.dot_general(a, b, (((1,), (1,)), ((), ())), preferred_element_type=F32)


def dot_tn(a, b):
    return lax.dot_general(a, b, (((0,), (0,)), ((), ())), preferred_element_type=F32)


def remote(src, dst, send, recv, device):
    return pltpu.make_async_remote_copy(
        src_ref=src, dst_ref=dst, send_sem=send, recv_sem=recv, device_id=device, device_id_type=MESH
    )


def exchange_kernel(
    pressure_h, prev_h, perm_h, uplus_h, uminus_h, state_h, cell_h, dest_h, target_h, source_h, mortar_h,
    faces_o, flow_o,
    pres, prev, perm, mort, flow, proj, slots_t, owner, weight, zsend, zrecv, csend, crecv, xsend, xrecv,
    tsend, trecv, rsend, rrecv, row_send, row_recv, col_send, col_recv, node_p,
    uplus_r, uminus_r, state_r, cell_r, dest_r, target_r, source_s, by_patch,
    fsem, msem, lsem, zss, zrs, css, crs, xss, xrs, tss, trs, rss, rrs, hss, hrs, osem,
):
    seg = lax.axis_index("seg")
    me = lax.axis_index("dev")
    n_seg = lax.axis_size("seg")
    n_dev = lax.axis_size("dev")
    z, pos = me // NP, lax.rem(me, NP)

    def column(p):
        return {"dev": z * NP + p}

    def row(zz):
        return {"dev": zz * NP + pos}

    seg_up, seg_down = {"seg": lax.rem(seg + 1, n_seg)}, {"seg": lax.rem(seg + n_seg - 1, n_seg)}
    dev_up, dev_down = {"dev": lax.rem(me + 1, n_dev)}, {"dev": lax.rem(me + n_dev - 1, n_dev)}

    def fetch(pairs, sems):
        copies = [pltpu.make_async_copy(a, b, sems.at[i]) for i, (a, b) in enumerate(pairs)]
        for copy in copies:
            copy.start()
        return copies

    first = fetch(((dest_h, dest_r), (target_h, target_r), (source_h, source_s), (uminus_h, uminus_r)), fsem)
    mcopies = fetch([(mortar_h.at[pl.ds(8 * g, 8)], mort.at[pl.ds(8 * g, 8)]) for g in range(8)], msem)
    lcopies = fetch(
        (
            (pressure_h, pres), (cell_h, cell_r), (perm_h, perm), (prev_h, prev),
            (uplus_h, uplus_r), (state_h, state_r),
        ),
        lsem,
    )

    barrier = pltpu.get_barrier_semaphore()
    for i in range(1, NP):
        pl.semaphore_signal(barrier, inc=1, device_id=column(lax.rem(pos + i, NP)), device_id_type=MESH)
    for i in range(1, NZ):
        pl.semaphore_signal(barrier, inc=1, device_id=row(lax.rem(z + i, NZ)), device_id_type=MESH)
    for device in (seg_up, seg_down, dev_up, dev_down):
        pl.semaphore_signal(barrier, inc=1, device_id=device, device_id_type=MESH)

    for copy in first:
        copy.wait()
    for b in range(8):
        for c in range(3):
            by_patch[b, c : c + 1, :] = uminus_r[c].astype(F32)[b : b + 1, :]

    lane, sub = iota((64, 128), 1), iota((64, 128), 0)
    diagonal = lane == sub

    def as_column(ref):
        wide = jnp.concatenate([ref[...].reshape(1, 64), jnp.full((1, 64), -1, I32)], axis=1)
        wide = jnp.broadcast_to(wide, (64, 128))
        return wide, jnp.sum(jnp.where(diagonal, wide, 0), axis=1, keepdims=True)

    dest_row, dest = as_column(dest_r)
    _, target = as_column(target_r)
    rank = jnp.sum(jnp.where((dest_row == dest) & (lane < sub), 1, 0), axis=1, keepdims=True)
    slot = ((dest & (NP - 1)) * NZ + (dest >> 3)) * CAP + rank
    for h in range(2):
        slots_t[:, 128 * h : 128 * (h + 1)] = jnp.where(slot == lane + 128 * h, 1.0, 0.0).astype(BF16)
    for g in range(8):
        mcopies[g].wait()

        def project(j, carry):
            q = 8 * g + j
            value = dot_nt(by_patch[source_s[q]].astype(BF16), mort[q])
            for c in range(3):
                proj[pl.ds(q, 1), 128 * c : 128 * (c + 1)] = value[c : c + 1, :]
            return carry

        lax.fori_loop(0, 8, project, 0, unroll=True)
    size = jnp.max(jnp.abs(proj[...]), axis=1, keepdims=True)
    power = jnp.floor(jnp.log2(jnp.maximum(size, 1e-30))) + 1.0
    whole = jnp.clip(jnp.round(proj[...] * jnp.exp2(15.0 - power)), -32767.0, 32767.0)
    label = target.astype(F32) + 8.0 * (power + 128.0)
    for p in range(NP):
        code = jnp.sum(jnp.where(slot == (lane & 31) + 32 * p, label, 0.0), axis=0, keepdims=True)
        csend[p] = jnp.broadcast_to(code, (8, 128))
    high, low = split2(whole)
    hit = slots_t[...]
    zsend[...] = (dot_tn(hit, high) + dot_tn(hit, low)).astype(I32).astype(I16).reshape(NP, 32, 384)

    pl.semaphore_wait(barrier, NP - 1 + NZ - 1 + 4)

    zcopies, ccopies = [], []
    for i in range(1, NP):
        p = lax.rem(pos + i, NP)
        ccopies.append(remote(csend.at[p], crecv.at[pos], css.at[i], crs.at[pos], column(p)))
        zcopies.append(remote(zsend.at[p], zrecv.at[pos], zss.at[i], zrs.at[pos], column(p)))
        ccopies[-1].start()
        zcopies[-1].start()
    crecv[pos] = csend[pos]
    zrecv[pos] = zsend[pos]

    for copy in lcopies:
        copy.wait()
    for b in range(4):
        cut = slice(128 * b, 128 * (b + 1))
        row_send[0, b : b + 1, :] = pres[0:1, cut]
        row_send[0, 4 + b : 5 + b, :] = perm[0:1, cut]
        row_send[1, b : b + 1, :] = pres[127:128, cut]
        row_send[1, 4 + b : 5 + b, :] = perm[127:128, cut]
    lane2 = iota((128, 128), 1)
    edge = jnp.where(
        lane2 == 0,
        pres[:, 0:128],
        jnp.where(
            lane2 == 1,
            pltpu.roll(perm[:, 0:128], 1, 1),
            jnp.where(lane2 == 127, pres[:, 384:512], pltpu.roll(perm[:, 384:512], 127, 1)),
        ),
    )
    edge = edge.T
    col_send[0] = edge[0:8, :]
    col_send[1] = edge[120:128, :]
    hcopies = [
        remote(row_send.at[0], row_recv.at[1], hss.at[0], hrs.at[0], seg_down),
        remote(row_send.at[1], row_recv.at[0], hss.at[1], hrs.at[1], seg_up),
        remote(col_send.at[0], col_recv.at[1], hss.at[2], hrs.at[2], dev_down),
        remote(col_send.at[1], col_recv.at[0], hss.at[3], hrs.at[3], dev_up),
    ]
    for copy in hcopies:
        copy.start()

    cell = cell_r[...]
    cell_lane, cell_block = cell & 127, cell >> 7

    def look(r, found):
        lines = pres[pl.ds(pl.multiple_of(8 * r, 8), 8), :]
        for i in range(8):
            for b in range(4):
                line = jnp.broadcast_to(lines[i : i + 1, 128 * b : 128 * (b + 1)], (8, 128))
                picked = jnp.take_along_axis(line, cell_lane, axis=1)
                found = jnp.where(cell_block == 32 * r + (4 * i + b), picked, found)
        return found

    node_p[...] = lax.fori_loop(0, 16, look, jnp.zeros((8, 128), F32))

    for i in range(1, NP):
        p = lax.rem(pos + i, NP)
        remote(csend.at[p], crecv.at[p], css.at[i], crs.at[p], column(p)).wait_recv()
        remote(zsend.at[p], zrecv.at[p], zss.at[i], zrs.at[p], column(p)).wait_recv()
    for h in range(2):
        code = jnp.zeros((8, 128), F32)
        for p in range(4):
            code = jnp.where((iota((8, 128), 1) >> 5) == p, crecv[4 * h + p], code)
        code = jnp.broadcast_to(code[0:1, :], (64, 128)).astype(I32)
        scale = jnp.exp2((code >> 3).astype(F32) - (128.0 + 15.0))
        match = ((code & 7) == (sub & 7)) & (((lane & 31) >> 2) == (sub >> 3))
        owner[:, 128 * h : 128 * (h + 1)] = jnp.where(match, 1.0, 0.0).astype(BF16)
        weight[:, 128 * h : 128 * (h + 1)] = jnp.where(match, scale, 0.0).astype(BF16)
    high, low = split2(zrecv[...].reshape(256, 384).astype(I32).astype(F32))
    weights = weight[...]
    dense = dot_nn(weights, high) + dot_nn(weights, low)
    xsend[...] = dense.reshape(NZ, 8, 384)
    xcopies = []
    for i in range(1, NZ):
        zz = lax.rem(z + i, NZ)
        xcopies.append(remote(xsend.at[zz], xrecv.at[z], xss.at[i], xrs.at[z], row(zz)))
        xcopies[-1].start()
    xrecv[z] = xsend[z]

    for i in range(4):
        hcopies[i].wait_recv()
    zero_row = jnp.zeros((1, 128), F32)
    above, below = [], []
    for half in range(2):
        for b in range(4):
            above.append(jnp.where(seg > 0, row_recv[0, 4 * half + b : 4 * half + b + 1, :], zero_row))
            below.append(jnp.where(seg < n_seg - 1, row_recv[1, 4 * half + b : 4 * half + b + 1, :], zero_row))
    pres_above, perm_above = jnp.concatenate(above[:4], axis=1), jnp.concatenate(above[4:], axis=1)
    pres_below, perm_below = jnp.concatenate(below[:4], axis=1), jnp.concatenate(below[4:], axis=1)
    sides = jnp.concatenate(
        [
            jnp.where(me > 0, col_recv[0], 0.0),
            jnp.where(me < n_dev - 1, col_recv[1], 0.0),
            jnp.zeros((112, 128), F32),
        ],
        axis=0,
    ).T
    lane8 = iota((8, 512), 1)

    def edge_term(p, k, p2, k2):
        return (2.0 * k * k2 / (k + k2)) * (p - p2)

    for r in range(16):
        rows = slice(8 * r, 8 * (r + 1))
        p, k = pres[rows, :], perm[rows, :]
        if r == 0:
            pu = jnp.concatenate([pres_above, pres[0:7, :]], axis=0)
            ku = jnp.concatenate([perm_above, perm[0:7, :]], axis=0)
        else:
            pu, ku = pres[8 * r - 1 : 8 * r + 7, :], perm[8 * r - 1 : 8 * r + 7, :]
        if r == 15:
            pd = jnp.concatenate([pres[121:128, :], pres_below], axis=0)
            kd = jnp.concatenate([perm[121:128, :], perm_below], axis=0)
        else:
            pd, kd = pres[8 * r + 1 : 8 * r + 9, :], perm[8 * r + 1 : 8 * r + 9, :]
        side = sides[rows, :]
        pl_, kl_ = side[:, 7:8], side[:, 6:7]
        pr_, kr_ = side[:, 8:9], side[:, 9:10]
        pleft = jnp.where(lane8 == 0, pl_, pltpu.roll(p, 1, 1))
        kleft = jnp.where(lane8 == 0, kl_, pltpu.roll(k, 1, 1))
        pright = jnp.where(lane8 == 511, pr_, pltpu.roll(p, 511, 1))
        kright = jnp.where(lane8 == 511, kr_, pltpu.roll(k, 511, 1))
        total = COMPRESS * (p - prev[rows, :])
        total = total + edge_term(p, k, pd, kd) + edge_term(p, k, pu, ku)
        total = total + edge_term(p, k, pright, kright) + edge_term(p, k, pleft, kleft)
        flow[rows, :] = total
    flow_copy = pltpu.make_async_copy(flow, flow_o, osem.at[0])
    flow_copy.start()

    for i in range(1, NZ):
        zz = lax.rem(z + i, NZ)
        remote(xsend.at[zz], xrecv.at[zz], xss.at[i], xrs.at[zz], row(zz)).wait_recv()
    mortar_sum = xrecv[0]
    for i in range(1, NZ):
        mortar_sum = mortar_sum + xrecv[i]
    jump = [uplus_r[c] - mortar_sum[:, 128 * c : 128 * (c + 1)] for c in range(3)]
    normal_part = PENALTY * jump[0]
    stress = CONFINING - node_p[...] - normal_part
    softplus = jnp.maximum(stress, 0.0) + jnp.log1p(jnp.exp(-jnp.abs(stress)))
    factor = FRICTION * softplus / jnp.sqrt(jump[1] * jump[1] + jump[2] * jump[2] + 1.0)
    state = state_r[...]
    sliding = [normal_part, jump[1] * factor, jump[2] * factor]
    traction = [
        jnp.where(state == 0, PENALTY * jump[c], jnp.where(state == 1, sliding[c], 0.0)) for c in range(3)
    ]
    for c in range(3):
        faces_o[c] = traction[c]
    tsend[...] = jnp.concatenate(traction + [jnp.zeros((8, 128), F32)], axis=0).astype(BF16)
    tcopies = []
    for i in range(1, NZ):
        zz = lax.rem(z + i, NZ)
        tcopies.append(remote(tsend, trecv.at[z], tss.at[i], trs.at[z], row(zz)))
        tcopies[-1].start()
    trecv[z] = tsend[...]
    for i in range(1, NZ):
        zz = lax.rem(z + i, NZ)
        remote(tsend, trecv.at[zz], tss.at[i], trs.at[zz], row(zz)).wait_recv()

    got = trecv[...].astype(F32)
    table = jnp.concatenate([got[:, 8 * c : 8 * (c + 1), :].reshape(64, 128) for c in range(3)], axis=1)
    rsend[...] = dot_tn(owner[...], table.astype(BF16)).astype(BF16).reshape(NP, 32, 384)
    rcopies = []
    for i in range(1, NP):
        p = lax.rem(pos + i, NP)
        rcopies.append(remote(rsend.at[p], rrecv.at[pos], rss.at[i], rrs.at[pos], column(p)))
        rcopies[-1].start()
    rrecv[pos] = rsend[pos]
    for i in range(1, NP):
        p = lax.rem(pos + i, NP)
        remote(rsend.at[p], rrecv.at[p], rss.at[i], rrs.at[p], column(p)).wait_recv()
    proj[...] = dot_nn(slots_t[...], rrecv[...].reshape(256, 384))

    patch = iota((8, 128), 0)
    total = jnp.zeros((32, 128), F32)
    for g in range(8):
        values = proj[8 * g : 8 * (g + 1), :]
        for j in range(8):
            q = 8 * g + j
            mine = patch == source_s[q]
            rows = [
                jnp.where(mine, jnp.broadcast_to(values[j : j + 1, 128 * c : 128 * (c + 1)], (8, 128)), 0.0)
                for c in range(3)
            ]
            left = jnp.concatenate(rows + [jnp.zeros((8, 128), F32)], axis=0).astype(BF16)
            total = total + dot_nn(left, mort[q])
    for c in range(3):
        faces_o[3 + c] = -total[8 * c : 8 * (c + 1), :]

    for copy in ccopies + zcopies + hcopies + xcopies + tcopies + rcopies:
        copy.wait_send()
    flow_copy.wait()


def store_kernel(faces_h, flow_h, flow_o, traction_o, force_o, faces, flow, lsem, osem):
    loads = [pltpu.make_async_copy(faces_h, faces, lsem.at[0]), pltpu.make_async_copy(flow_h, flow, lsem.at[1])]
    stores = [
        pltpu.make_async_copy(faces.at[pl.ds(0, 3)], traction_o, osem.at[0]),
        pltpu.make_async_copy(faces.at[pl.ds(3, 3)], force_o, osem.at[1]),
        pltpu.make_async_copy(flow, flow_o, osem.at[2]),
    ]
    for copy in loads:
        copy.start()
    loads[0].wait()
    stores[0].start()
    stores[1].start()
    loads[1].wait()
    stores[2].start()
    for copy in stores:
        copy.wait()


def on_device(
    pressure, pressure_prev, permeability, u_plus, u_minus, node_state, node_cell,
    pair_source, pair_dest, pair_target, mortar,
):
    hbm, vmem = (pl.BlockSpec(memory_space=s) for s in (pltpu.HBM, pltpu.VMEM))
    dma = pltpu.SemaphoreType.DMA
    shape = jax.ShapeDtypeStruct
    faces, flow = pl.pallas_call(
        exchange_kernel,
        out_shape=(shape((6, 8, 128), F32), shape((128, 512), F32)),
        in_specs=[hbm] * 11,
        out_specs=(vmem, hbm),
        scratch_shapes=[
            pltpu.VMEM((128, 512), F32),
            pltpu.VMEM((128, 512), F32),
            pltpu.VMEM((128, 512), F32),
            pltpu.VMEM((64, 128, 128), BF16),
            pltpu.VMEM((128, 512), F32),
            pltpu.VMEM((64, 384), F32),
            pltpu.VMEM((64, 256), BF16),
            pltpu.VMEM((64, 256), BF16),
            pltpu.VMEM((64, 256), BF16),
            pltpu.VMEM((NP, 32, 384), I16),
            pltpu.VMEM((NP, 32, 384), I16),
            pltpu.VMEM((NP, 8, 128), F32),
            pltpu.VMEM((NP, 8, 128), F32),
            pltpu.VMEM((NZ, 8, 384), F32),
            pltpu.VMEM((NZ, 8, 384), F32),
            pltpu.VMEM((32, 128), BF16),
            pltpu.VMEM((NZ, 32, 128), BF16),
            pltpu.VMEM((NP, 32, 384), BF16),
            pltpu.VMEM((NP, 32, 384), BF16),
            pltpu.VMEM((2, 8, 128), F32),
            pltpu.VMEM((2, 8, 128), F32),
            pltpu.VMEM((2, 8, 128), F32),
            pltpu.VMEM((2, 8, 128), F32),
            pltpu.VMEM((8, 128), F32),
            pltpu.VMEM((3, 8, 128), F32),
            pltpu.VMEM((3, 8, 128), BF16),
            pltpu.VMEM((8, 128), I32),
            pltpu.VMEM((8, 128), I32),
            pltpu.VMEM((64,), I32),
            pltpu.VMEM((64,), I32),
            pltpu.SMEM((64,), I32),
            pltpu.VMEM((8, 8, 128), F32),
            dma((4,)), dma((8,)), dma((6,)),
            dma((8,)), dma((8,)), dma((8,)), dma((8,)), dma((8,)), dma((8,)),
            dma((8,)), dma((8,)), dma((8,)), dma((8,)), dma((4,)), dma((4,)), dma((1,)),
        ],
        compiler_params=pltpu.CompilerParams(
            collective_id=0, has_side_effects=True, vmem_limit_bytes=60 * 1024 * 1024
        ),
        name="exchange",
    )(
        pressure, pressure_prev, permeability, u_plus.transpose(1, 0, 2), u_minus.transpose(1, 0, 2),
        node_state, node_cell, pair_dest.reshape(64), pair_target, pair_source, mortar,
    )
    flow, traction, force = pl.pallas_call(
        store_kernel,
        out_shape=(shape((128, 512), F32), shape((3, 8, 128), F32), shape((3, 8, 128), F32)),
        in_specs=[hbm, hbm],
        out_specs=(hbm, hbm, hbm),
        scratch_shapes=[pltpu.VMEM((6, 8, 128), F32), pltpu.VMEM((128, 512), F32), dma((2,)), dma((3,))],
        compiler_params=pltpu.CompilerParams(vmem_limit_bytes=60 * 1024 * 1024),
        name="store",
    )(faces, flow)
    return flow, traction.transpose(1, 0, 2), force.transpose(1, 0, 2)


def solution(mesh):
    both = ("seg", "dev")
    cells, patches = P("seg", "dev"), P(both, None, None)
    placed = (
        cells, cells, cells, patches, patches, P(both, None), P(both, None), P(both), P(both, None), P(both), patches,
    )
    return jax.shard_map(
        on_device, mesh=mesh, in_specs=placed, out_specs=(cells, patches, patches), check_vma=False
    )
```

```python
import jax
import jax.numpy as jnp
from jax import lax
from jax.experimental import pallas as pl
from jax.experimental.pallas import tpu as pltpu
from jax.sharding import PartitionSpec as P

CAP = 4
COMPRESS = 0.5
PENALTY = 1.5
FRICTION = 0.6
CONFINING = 1.0

NP = 8
NZ = 8
FAR = (4, 3, 5, 2, 6, 1, 7, 0)
COLUMN_ORDER = (4, 5, 3, 2, 6, 1, 7)
HALF = NP * 16
F32 = jnp.float32
BF16 = jnp.bfloat16
I32 = jnp.int32
I16 = jnp.int16
MESH = pl.DeviceIdType.MESH


def iota(shape, dim):
    return lax.broadcasted_iota(I32, shape, dim)


def split2(value):
    high = value.astype(BF16)
    return high, (value - high.astype(F32)).astype(BF16)


def dot_nn(a, b):
    return lax.dot_general(a, b, (((1,), (0,)), ((), ())), preferred_element_type=F32)


def dot_nt(a, b):
    return lax.dot_general(a, b, (((1,), (1,)), ((), ())), preferred_element_type=F32)


def dot_tn(a, b):
    return lax.dot_general(a, b, (((0,), (0,)), ((), ())), preferred_element_type=F32)


def remote(src, dst, send, recv, device):
    return pltpu.make_async_remote_copy(
        src_ref=src, dst_ref=dst, send_sem=send, recv_sem=recv, device_id=device, device_id_type=MESH
    )


def exchange_kernel(
    pressure_h, prev_h, perm_h, uplus_h, uminus_h, state_h, cell_h, dest_h, target_h, source_h, mortar_h,
    faces_o, flow_o,
    pres, prev, perm, mort, flow, proj, slots_t, owner, zsend, zrecv, csend, crecv, xsend, xrecv,
    tsend, trecv, rsend, rrecv, row_send, row_recv, col_send, col_recv, node_p,
    uplus_r, uminus_r, state_r, cell_r, dest_r, target_r, source_s, by_patch,
    fsem, msem, lsem, zss, zrs, css, crs, xss, xrs, tss, trs, rss, rrs, hss, hrs, osem,
):
    seg = lax.axis_index("seg")
    me = lax.axis_index("dev")
    n_seg = lax.axis_size("seg")
    n_dev = lax.axis_size("dev")
    z, pos = me // NP, lax.rem(me, NP)

    def column(p):
        return {"dev": z * NP + p}

    def row(zz):
        return {"dev": zz * NP + pos}

    seg_up, seg_down = {"seg": lax.rem(seg + 1, n_seg)}, {"seg": lax.rem(seg + n_seg - 1, n_seg)}
    dev_up, dev_down = {"dev": lax.rem(me + 1, n_dev)}, {"dev": lax.rem(me + n_dev - 1, n_dev)}

    barrier = pltpu.get_barrier_semaphore()
    neighbours = [column(lax.rem(pos + i, NP)) for i in COLUMN_ORDER]
    neighbours += [row(lax.rem(z + i, NZ)) for i in FAR[:7]]
    neighbours += [seg_up, seg_down, dev_up, dev_down]
    for device in neighbours:
        pl.semaphore_signal(barrier, inc=1, device_id=device, device_id_type=MESH)

    def fetch(pairs, sems):
        copies = [pltpu.make_async_copy(a, b, sems.at[i]) for i, (a, b) in enumerate(pairs)]
        for copy in copies:
            copy.start()
        return copies

    first = fetch(((dest_h, dest_r), (target_h, target_r), (source_h, source_s), (uminus_h, uminus_r)), fsem)
    mcopies = fetch([(mortar_h.at[pl.ds(8 * g, 8)], mort.at[pl.ds(8 * g, 8)]) for g in range(8)], msem)
    lcopies = fetch(
        (
            (pressure_h, pres), (cell_h, cell_r), (perm_h, perm), (prev_h, prev),
            (uplus_h, uplus_r), (state_h, state_r),
        ),
        lsem,
    )

    for copy in first:
        copy.wait()
    by_patch[...] = jnp.zeros_like(by_patch)
    for b in range(8):
        for c in range(3):
            by_patch[0, b, c : c + 1, :] = uminus_r[c].astype(F32)[b : b + 1, :]
            by_patch[1, b, 4 + c : 5 + c, :] = uminus_r[c].astype(F32)[b : b + 1, :]

    lane, sub = iota((64, 128), 1), iota((64, 128), 0)
    diagonal = lane == sub

    def as_column(ref):
        wide = jnp.concatenate([ref[...].reshape(1, 64), jnp.full((1, 64), -1, I32)], axis=1)
        wide = jnp.broadcast_to(wide, (64, 128))
        return wide, jnp.sum(jnp.where(diagonal, wide, 0), axis=1, keepdims=True)

    dest_row, dest = as_column(dest_r)
    _, target = as_column(target_r)
    rank = jnp.sum(jnp.where((dest_row == dest) & (lane < sub), 1, 0), axis=1, keepdims=True)
    distance = ((dest >> 3) + NZ - z) & (NZ - 1)
    turn = jnp.zeros((64, 1), I32)
    for i in range(NZ):
        turn = jnp.where(distance == FAR[i], i, turn)
    slot = (turn >> 2) * HALF + (dest & (NP - 1)) * 16 + (turn & 3) * CAP + rank
    for h in range(2):
        slots_t[:, 128 * h : 128 * (h + 1)] = jnp.where(slot == lane + 128 * h, 1.0, 0.0).astype(BF16)
    for g in range(8):
        mcopies[g].wait()
        lines = [[], [], []]
        for j in range(0, 8, 2):
            q = 8 * g + j
            left = (by_patch[0, source_s[q]] + by_patch[1, source_s[q + 1]]).astype(BF16)
            value = dot_nt(left, mort[q : q + 2].reshape(256, 128))
            for c in range(3):
                lines[c] += [value[c : c + 1, 0:128], value[4 + c : 5 + c, 128:256]]
        for c in range(3):
            proj[8 * g : 8 * (g + 1), 128 * c : 128 * (c + 1)] = jnp.concatenate(lines[c], axis=0)
    size = jnp.max(jnp.abs(proj[...]), axis=1, keepdims=True)
    power = jnp.floor(jnp.log2(jnp.maximum(size, 1e-30))) + 1.0
    whole = jnp.clip(jnp.round(proj[...] * jnp.exp2(15.0 - power)), -32767.0, 32767.0)
    label = target.astype(F32) + 8.0 * (power + 128.0)
    for p in range(NP):
        for h in range(2):
            spot = slot == (lane & 15) + (h * HALF + 16 * p)
            csend[p, h : h + 1, :] = jnp.sum(jnp.where(spot, label, 0.0), axis=0, keepdims=True)
    high, low = split2(whole)

    def place(h):
        hit = slots_t[:, HALF * h : HALF * (h + 1)]
        zsend[h] = (dot_tn(hit, high) + dot_tn(hit, low)).astype(I32).astype(I16).reshape(NP, 16, 384)

    place(0)
    pl.semaphore_wait(barrier, len(neighbours))

    ccopies, zcopies = [], []
    for i in COLUMN_ORDER:
        p = lax.rem(pos + i, NP)
        ccopies.append(remote(csend.at[p], crecv.at[pos], css.at[i], crs.at[pos], column(p)))
        zcopies.append(remote(zsend.at[0, p], zrecv.at[0, pos], zss.at[0, i], zrs.at[0, pos], column(p)))
        ccopies[-1].start()
        zcopies[-1].start()
    place(1)
    for i in COLUMN_ORDER:
        p = lax.rem(pos + i, NP)
        zcopies.append(remote(zsend.at[1, p], zrecv.at[1, pos], zss.at[1, i], zrs.at[1, pos], column(p)))
        zcopies[-1].start()
    crecv[pos] = csend[pos]
    for h in range(2):
        zrecv[h, pos] = zsend[h, pos]

    for copy in lcopies:
        copy.wait()
    for b in range(4):
        cut = slice(128 * b, 128 * (b + 1))
        row_send[0, b : b + 1, :] = pres[0:1, cut]
        row_send[0, 4 + b : 5 + b, :] = perm[0:1, cut]
        row_send[1, b : b + 1, :] = pres[127:128, cut]
        row_send[1, 4 + b : 5 + b, :] = perm[127:128, cut]
    lane2 = iota((128, 128), 1)
    edge = jnp.where(
        lane2 == 0,
        pres[:, 0:128],
        jnp.where(
            lane2 == 1,
            pltpu.roll(perm[:, 0:128], 1, 1),
            jnp.where(lane2 == 127, pres[:, 384:512], pltpu.roll(perm[:, 384:512], 127, 1)),
        ),
    )
    edge = edge.T
    col_send[0] = edge[0:8, :]
    col_send[1] = edge[120:128, :]
    hcopies = [
        remote(row_send.at[0], row_recv.at[1], hss.at[0], hrs.at[0], seg_down),
        remote(row_send.at[1], row_recv.at[0], hss.at[1], hrs.at[1], seg_up),
        remote(col_send.at[0], col_recv.at[1], hss.at[2], hrs.at[2], dev_down),
        remote(col_send.at[1], col_recv.at[0], hss.at[3], hrs.at[3], dev_up),
    ]
    for copy in hcopies:
        copy.start()

    cell = cell_r[...]
    cell_lane, cell_block = cell & 127, cell >> 7

    def look(r, found):
        lines = pres[pl.ds(pl.multiple_of(8 * r, 8), 8), :]
        for i in range(8):
            for b in range(4):
                line = jnp.broadcast_to(lines[i : i + 1, 128 * b : 128 * (b + 1)], (8, 128))
                picked = jnp.take_along_axis(line, cell_lane, axis=1)
                found = jnp.where(cell_block == 32 * r + (4 * i + b), picked, found)
        return found

    node_p[...] = lax.fori_loop(0, 16, look, jnp.zeros((8, 128), F32))

    for i in COLUMN_ORDER:
        p = lax.rem(pos + i, NP)
        remote(csend.at[p], crecv.at[p], css.at[i], crs.at[p], column(p)).wait_recv()
    lane32, sub32 = iota((32, 128), 1), iota((32, 128), 0)
    in_turn = ((lane32 & 15) >> 2) == (sub32 >> 3)
    codes = crecv[0]
    for p in range(1, NP):
        codes = jnp.where((iota((8, 128), 1) >> 4) == p, crecv[p], codes)
    xcopies = []
    for h in range(2):
        code = jnp.broadcast_to(codes[h : h + 1, :], (32, 128)).astype(I32)
        scale = jnp.exp2((code >> 3).astype(F32) - (128.0 + 15.0))
        match = ((code & 7) == (sub32 & 7)) & in_turn
        owner[h] = jnp.where(match, 1.0, 0.0).astype(BF16)
        weight = jnp.where(match, scale, 0.0).astype(BF16)
        for i in COLUMN_ORDER:
            p = lax.rem(pos + i, NP)
            remote(zsend.at[h, p], zrecv.at[h, p], zss.at[h, i], zrs.at[h, p], column(p)).wait_recv()
        high, low = split2(zrecv[h].reshape(HALF, 384).astype(I32).astype(F32))
        xsend[4 * h : 4 * (h + 1)] = (dot_nn(weight, high) + dot_nn(weight, low)).reshape(4, 8, 384)
        for i in range(4 * h, min(4 * h + 4, NZ - 1)):
            there, back = row(lax.rem(z + FAR[i], NZ)), FAR.index((NZ - FAR[i]) % NZ)
            xcopies.append(remote(xsend.at[i], xrecv.at[back], xss.at[i], xrs.at[back], there))
            xcopies[-1].start()

    for i in range(4):
        hcopies[i].wait_recv()
    zero_row = jnp.zeros((1, 128), F32)
    above, below = [], []
    for half in range(2):
        for b in range(4):
            above.append(jnp.where(seg > 0, row_recv[0, 4 * half + b : 4 * half + b + 1, :], zero_row))
            below.append(jnp.where(seg < n_seg - 1, row_recv[1, 4 * half + b : 4 * half + b + 1, :], zero_row))
    pres_above, perm_above = jnp.concatenate(above[:4], axis=1), jnp.concatenate(above[4:], axis=1)
    pres_below, perm_below = jnp.concatenate(below[:4], axis=1), jnp.concatenate(below[4:], axis=1)
    sides = jnp.concatenate(
        [
            jnp.where(me > 0, col_recv[0], 0.0),
            jnp.where(me < n_dev - 1, col_recv[1], 0.0),
            jnp.zeros((112, 128), F32),
        ],
        axis=0,
    ).T
    lane8 = iota((8, 512), 1)

    def edge_term(p, k, p2, k2):
        return (2.0 * k * k2 / (k + k2)) * (p - p2)

    for r in range(16):
        rows = slice(8 * r, 8 * (r + 1))
        p, k = pres[rows, :], perm[rows, :]
        if r == 0:
            pu = jnp.concatenate([pres_above, pres[0:7, :]], axis=0)
            ku = jnp.concatenate([perm_above, perm[0:7, :]], axis=0)
        else:
            pu, ku = pres[8 * r - 1 : 8 * r + 7, :], perm[8 * r - 1 : 8 * r + 7, :]
        if r == 15:
            pd = jnp.concatenate([pres[121:128, :], pres_below], axis=0)
            kd = jnp.concatenate([perm[121:128, :], perm_below], axis=0)
        else:
            pd, kd = pres[8 * r + 1 : 8 * r + 9, :], perm[8 * r + 1 : 8 * r + 9, :]
        side = sides[rows, :]
        pl_, kl_ = side[:, 7:8], side[:, 6:7]
        pr_, kr_ = side[:, 8:9], side[:, 9:10]
        pleft = jnp.where(lane8 == 0, pl_, pltpu.roll(p, 1, 1))
        kleft = jnp.where(lane8 == 0, kl_, pltpu.roll(k, 1, 1))
        pright = jnp.where(lane8 == 511, pr_, pltpu.roll(p, 511, 1))
        kright = jnp.where(lane8 == 511, kr_, pltpu.roll(k, 511, 1))
        total = COMPRESS * (p - prev[rows, :])
        total = total + edge_term(p, k, pd, kd) + edge_term(p, k, pu, ku)
        total = total + edge_term(p, k, pright, kright) + edge_term(p, k, pleft, kleft)
        flow[rows, :] = total
    flow_copy = pltpu.make_async_copy(flow, flow_o, osem.at[0])
    flow_copy.start()

    mortar_sum = xsend[NZ - 1]
    for i in range(NZ - 2, -1, -1):
        remote(xsend.at[i], xrecv.at[i], xss.at[i], xrs.at[i], row(lax.rem(z + FAR[i], NZ))).wait_recv()
        mortar_sum = mortar_sum + xrecv[i]
    jump = [uplus_r[c] - mortar_sum[:, 128 * c : 128 * (c + 1)] for c in range(3)]
    normal_part = PENALTY * jump[0]
    stress = CONFINING - node_p[...] - normal_part
    softplus = jnp.maximum(stress, 0.0) + jnp.log1p(jnp.exp(-jnp.abs(stress)))
    factor = FRICTION * softplus / jnp.sqrt(jump[1] * jump[1] + jump[2] * jump[2] + 1.0)
    state = state_r[...]
    sliding = [normal_part, jump[1] * factor, jump[2] * factor]
    traction = [
        jnp.where(state == 0, PENALTY * jump[c], jnp.where(state == 1, sliding[c], 0.0)) for c in range(3)
    ]
    tsend[...] = jnp.concatenate(traction + [jnp.zeros((8, 128), F32)], axis=0).astype(BF16)
    tcopies = []
    for i in range(NZ - 1):
        there, back = row(lax.rem(z + FAR[i], NZ)), FAR.index((NZ - FAR[i]) % NZ)
        tcopies.append(remote(tsend, trecv.at[back], tss.at[i], trs.at[back], there))
        tcopies[-1].start()
    trecv[NZ - 1] = tsend[...]
    for c in range(3):
        faces_o[c] = traction[c]

    rcopies = []
    for h in (1, 0):
        for i in range(min(4 * h + 3, NZ - 2), 4 * h - 1, -1):
            remote(tsend, trecv.at[i], tss.at[i], trs.at[i], row(lax.rem(z + FAR[i], NZ))).wait_recv()
        got = trecv[4 * h : 4 * (h + 1)].astype(F32)
        table = jnp.concatenate([got[:, 8 * c : 8 * (c + 1), :].reshape(32, 128) for c in range(3)], axis=1)
        rsend[h] = dot_tn(owner[h], table.astype(BF16)).astype(BF16).reshape(NP, 16, 384)
        for i in COLUMN_ORDER:
            p = lax.rem(pos + i, NP)
            rcopies.append(remote(rsend.at[h, p], rrecv.at[h, pos], rss.at[h, i], rrs.at[h, pos], column(p)))
            rcopies[-1].start()
        rrecv[h, pos] = rsend[h, pos]
    replies = jnp.zeros((64, 384), F32)
    for h in (1, 0):
        for i in COLUMN_ORDER:
            p = lax.rem(pos + i, NP)
            remote(rsend.at[h, p], rrecv.at[h, p], rss.at[h, i], rrs.at[h, p], column(p)).wait_recv()
        replies = replies + dot_nn(slots_t[:, HALF * h : HALF * (h + 1)], rrecv[h].reshape(HALF, 384))

    patch = iota((8, 128), 0)
    total = jnp.zeros((32, 128), F32)
    for q in range(0, 64, 2):
        left = []
        for k in range(2):
            mine = patch == source_s[q + k]
            rows = [
                jnp.where(mine, jnp.broadcast_to(replies[q + k : q + k + 1, 128 * c : 128 * (c + 1)], (8, 128)), 0.0)
                for c in range(3)
            ]
            left.append(jnp.concatenate(rows + [jnp.zeros((8, 128), F32)], axis=0).astype(BF16))
        total = total + dot_nn(jnp.concatenate(left, axis=1), mort[q : q + 2].reshape(256, 128))
    for c in range(3):
        faces_o[3 + c] = -total[8 * c : 8 * (c + 1), :]

    for copy in ccopies + zcopies + hcopies + xcopies + tcopies + rcopies:
        copy.wait_send()
    flow_copy.wait()


def store_kernel(faces_h, flow_h, flow_o, traction_o, force_o, faces, flow, lsem, osem):
    loads = [pltpu.make_async_copy(faces_h, faces, lsem.at[0]), pltpu.make_async_copy(flow_h, flow, lsem.at[1])]
    stores = [
        pltpu.make_async_copy(faces.at[pl.ds(0, 3)], traction_o, osem.at[0]),
        pltpu.make_async_copy(faces.at[pl.ds(3, 3)], force_o, osem.at[1]),
        pltpu.make_async_copy(flow, flow_o, osem.at[2]),
    ]
    for copy in loads:
        copy.start()
    loads[0].wait()
    stores[0].start()
    stores[1].start()
    loads[1].wait()
    stores[2].start()
    for copy in stores:
        copy.wait()


def on_device(
    pressure, pressure_prev, permeability, u_plus, u_minus, node_state, node_cell,
    pair_source, pair_dest, pair_target, mortar,
):
    hbm, vmem = (pl.BlockSpec(memory_space=s) for s in (pltpu.HBM, pltpu.VMEM))
    dma = pltpu.SemaphoreType.DMA
    shape = jax.ShapeDtypeStruct
    faces, flow = pl.pallas_call(
        exchange_kernel,
        out_shape=(shape((6, 8, 128), F32), shape((128, 512), F32)),
        in_specs=[hbm] * 11,
        out_specs=(vmem, hbm),
        scratch_shapes=[
            pltpu.VMEM((128, 512), F32),
            pltpu.VMEM((128, 512), F32),
            pltpu.VMEM((128, 512), F32),
            pltpu.VMEM((64, 128, 128), BF16),
            pltpu.VMEM((128, 512), F32),
            pltpu.VMEM((64, 384), F32),
            pltpu.VMEM((64, 256), BF16),
            pltpu.VMEM((2, 32, HALF), BF16),
            pltpu.VMEM((2, NP, 16, 384), I16),
            pltpu.VMEM((2, NP, 16, 384), I16),
            pltpu.VMEM((NP, 8, 128), F32),
            pltpu.VMEM((NP, 8, 128), F32),
            pltpu.VMEM((NZ, 8, 384), F32),
            pltpu.VMEM((NZ, 8, 384), F32),
            pltpu.VMEM((32, 128), BF16),
            pltpu.VMEM((NZ, 32, 128), BF16),
            pltpu.VMEM((2, NP, 16, 384), BF16),
            pltpu.VMEM((2, NP, 16, 384), BF16),
            pltpu.VMEM((2, 8, 128), F32),
            pltpu.VMEM((2, 8, 128), F32),
            pltpu.VMEM((2, 8, 128), F32),
            pltpu.VMEM((2, 8, 128), F32),
            pltpu.VMEM((8, 128), F32),
            pltpu.VMEM((3, 8, 128), F32),
            pltpu.VMEM((3, 8, 128), BF16),
            pltpu.VMEM((8, 128), I32),
            pltpu.VMEM((8, 128), I32),
            pltpu.VMEM((64,), I32),
            pltpu.VMEM((64,), I32),
            pltpu.SMEM((64,), I32),
            pltpu.VMEM((2, 8, 8, 128), F32),
            dma((4,)), dma((8,)), dma((6,)),
            dma((2, 8)), dma((2, 8)), dma((8,)), dma((8,)), dma((8,)), dma((8,)),
            dma((8,)), dma((8,)), dma((2, 8)), dma((2, 8)), dma((4,)), dma((4,)), dma((1,)),
        ],
        compiler_params=pltpu.CompilerParams(
            collective_id=0, has_side_effects=True, vmem_limit_bytes=60 * 1024 * 1024
        ),
        name="exchange",
    )(
        pressure, pressure_prev, permeability, u_plus.transpose(1, 0, 2), u_minus.transpose(1, 0, 2),
        node_state, node_cell, pair_dest.reshape(64), pair_target, pair_source, mortar,
    )
    flow, traction, force = pl.pallas_call(
        store_kernel,
        out_shape=(shape((128, 512), F32), shape((3, 8, 128), F32), shape((3, 8, 128), F32)),
        in_specs=[hbm, hbm],
        out_specs=(hbm, hbm, hbm),
        scratch_shapes=[pltpu.VMEM((6, 8, 128), F32), pltpu.VMEM((128, 512), F32), dma((2,)), dma((3,))],
        compiler_params=pltpu.CompilerParams(vmem_limit_bytes=60 * 1024 * 1024),
        name="store",
    )(faces, flow)
    return flow, traction.transpose(1, 0, 2), force.transpose(1, 0, 2)


def solution(mesh):
    both = ("seg", "dev")
    cells, patches = P("seg", "dev"), P(both, None, None)
    placed = (
        cells, cells, cells, patches, patches, P(both, None), P(both, None), P(both), P(both, None), P(both), patches,
    )
    return jax.shard_map(
        on_device, mesh=mesh, in_specs=placed, out_specs=(cells, patches, patches), check_vma=False
    )
```

```python
import jax
import jax.numpy as jnp
from jax import lax
from jax.experimental import pallas as pl
from jax.experimental.pallas import tpu as pltpu
from jax.sharding import PartitionSpec as P

CAP = 4
COMPRESS = 0.5
PENALTY = 1.5
FRICTION = 0.6
CONFINING = 1.0

NP = 8
NZ = 8
FAR = (4, 3, 5, 2, 6, 1, 7, 0)
COLUMN_ORDER = (4, 5, 3, 2, 6, 1, 7)
HALF = NP * 16
F32 = jnp.float32
BF16 = jnp.bfloat16
I32 = jnp.int32
I16 = jnp.int16
MESH = pl.DeviceIdType.MESH


def iota(shape, dim):
    return lax.broadcasted_iota(I32, shape, dim)


def split2(value):
    high = value.astype(BF16)
    return high, (value - high.astype(F32)).astype(BF16)


def dot_nn(a, b):
    return lax.dot_general(a, b, (((1,), (0,)), ((), ())), preferred_element_type=F32)


def dot_nt(a, b):
    return lax.dot_general(a, b, (((1,), (1,)), ((), ())), preferred_element_type=F32)


def dot_tn(a, b):
    return lax.dot_general(a, b, (((0,), (0,)), ((), ())), preferred_element_type=F32)


def remote(src, dst, send, recv, device):
    return pltpu.make_async_remote_copy(
        src_ref=src, dst_ref=dst, send_sem=send, recv_sem=recv, device_id=device, device_id_type=MESH
    )


def exchange_kernel(
    pressure_h, prev_h, perm_h, uplus_h, uminus_h, state_h, cell_h, dest_h, target_h, source_h, mortar_h,
    faces_o, flow_o,
    pres, prev, perm, mort, proj, slots_t, owner, zsend, zrecv, csend, crecv, xsend, xrecv,
    tsend, trecv, rsend, rrecv, row_send, row_recv, col_send, col_recv, node_p,
    uplus_r, uminus_r, state_r, cell_r, dest_r, target_r, source_s, by_patch,
    fsem, msem, lsem, zss, zrs, css, crs, xss, xrs, tss, trs, rss, rrs, hss, hrs,
):
    seg = lax.axis_index("seg")
    me = lax.axis_index("dev")
    n_seg = lax.axis_size("seg")
    n_dev = lax.axis_size("dev")
    z, pos = me // NP, lax.rem(me, NP)

    def column(p):
        return {"dev": z * NP + p}

    def row(zz):
        return {"dev": zz * NP + pos}

    seg_up, seg_down = {"seg": lax.rem(seg + 1, n_seg)}, {"seg": lax.rem(seg + n_seg - 1, n_seg)}
    dev_up, dev_down = {"dev": lax.rem(me + 1, n_dev)}, {"dev": lax.rem(me + n_dev - 1, n_dev)}

    barrier = pltpu.get_barrier_semaphore()
    neighbours = [column(lax.rem(pos + i, NP)) for i in COLUMN_ORDER]
    neighbours += [row(lax.rem(z + i, NZ)) for i in FAR[:7]]
    neighbours += [seg_up, seg_down, dev_up, dev_down]
    for device in neighbours:
        pl.semaphore_signal(barrier, inc=1, device_id=device, device_id_type=MESH)

    def fetch(pairs, sems):
        copies = [pltpu.make_async_copy(a, b, sems.at[i]) for i, (a, b) in enumerate(pairs)]
        for copy in copies:
            copy.start()
        return copies

    first = fetch(((dest_h, dest_r), (target_h, target_r), (source_h, source_s), (uminus_h, uminus_r)), fsem)
    mcopies = fetch([(mortar_h.at[pl.ds(8 * g, 8)], mort.at[pl.ds(8 * g, 8)]) for g in range(8)], msem)
    lcopies = fetch(
        (
            (pressure_h, pres), (cell_h, cell_r), (perm_h, perm), (prev_h, prev),
            (uplus_h, uplus_r), (state_h, state_r),
        ),
        lsem,
    )

    for copy in first:
        copy.wait()
    by_patch[...] = jnp.zeros_like(by_patch)
    for b in range(8):
        for c in range(3):
            by_patch[0, b, c : c + 1, :] = uminus_r[c].astype(F32)[b : b + 1, :]
            by_patch[1, b, 4 + c : 5 + c, :] = uminus_r[c].astype(F32)[b : b + 1, :]

    lane, sub = iota((64, 128), 1), iota((64, 128), 0)
    diagonal = lane == sub

    def as_column(ref):
        wide = jnp.concatenate([ref[...].reshape(1, 64), jnp.full((1, 64), -1, I32)], axis=1)
        wide = jnp.broadcast_to(wide, (64, 128))
        return wide, jnp.sum(jnp.where(diagonal, wide, 0), axis=1, keepdims=True)

    dest_row, dest = as_column(dest_r)
    _, target = as_column(target_r)
    rank = jnp.sum(jnp.where((dest_row == dest) & (lane < sub), 1, 0), axis=1, keepdims=True)
    distance = ((dest >> 3) + NZ - z) & (NZ - 1)
    turn = jnp.zeros((64, 1), I32)
    for i in range(NZ):
        turn = jnp.where(distance == FAR[i], i, turn)
    slot = (turn >> 2) * HALF + (dest & (NP - 1)) * 16 + (turn & 3) * CAP + rank
    for h in range(2):
        slots_t[:, 128 * h : 128 * (h + 1)] = jnp.where(slot == lane + 128 * h, 1.0, 0.0).astype(BF16)
    for g in range(8):
        mcopies[g].wait()
        lines = [[], [], []]
        for j in range(0, 8, 2):
            q = 8 * g + j
            left = (by_patch[0, source_s[q]] + by_patch[1, source_s[q + 1]]).astype(BF16)
            value = dot_nt(left, mort[q : q + 2].reshape(256, 128))
            for c in range(3):
                lines[c] += [value[c : c + 1, 0:128], value[4 + c : 5 + c, 128:256]]
        for c in range(3):
            proj[8 * g : 8 * (g + 1), 128 * c : 128 * (c + 1)] = jnp.concatenate(lines[c], axis=0)
    size = jnp.max(jnp.abs(proj[...]), axis=1, keepdims=True)
    power = jnp.floor(jnp.log2(jnp.maximum(size, 1e-30))) + 1.0
    whole = jnp.clip(jnp.round(proj[...] * jnp.exp2(15.0 - power)), -32767.0, 32767.0)
    label = target.astype(F32) + 8.0 * (power + 128.0)
    for p in range(NP):
        for h in range(2):
            spot = slot == (lane & 15) + (h * HALF + 16 * p)
            csend[p, h : h + 1, :] = jnp.sum(jnp.where(spot, label, 0.0), axis=0, keepdims=True)
    high, low = split2(whole)

    def place(h):
        hit = slots_t[:, HALF * h : HALF * (h + 1)]
        zsend[h] = (dot_tn(hit, high) + dot_tn(hit, low)).astype(I32).astype(I16).reshape(NP, 16, 384)

    place(0)
    pl.semaphore_wait(barrier, len(neighbours))

    ccopies, zcopies = [], []
    for i in COLUMN_ORDER:
        p = lax.rem(pos + i, NP)
        ccopies.append(remote(csend.at[p], crecv.at[pos], css.at[i], crs.at[pos], column(p)))
        zcopies.append(remote(zsend.at[0, p], zrecv.at[0, pos], zss.at[0, i], zrs.at[0, pos], column(p)))
        ccopies[-1].start()
        zcopies[-1].start()
    place(1)
    for i in COLUMN_ORDER:
        p = lax.rem(pos + i, NP)
        zcopies.append(remote(zsend.at[1, p], zrecv.at[1, pos], zss.at[1, i], zrs.at[1, pos], column(p)))
        zcopies[-1].start()
    crecv[pos] = csend[pos]
    for h in range(2):
        zrecv[h, pos] = zsend[h, pos]

    for copy in lcopies:
        copy.wait()
    for b in range(4):
        cut = slice(128 * b, 128 * (b + 1))
        row_send[0, b : b + 1, :] = pres[0:1, cut]
        row_send[0, 4 + b : 5 + b, :] = perm[0:1, cut]
        row_send[1, b : b + 1, :] = pres[127:128, cut]
        row_send[1, 4 + b : 5 + b, :] = perm[127:128, cut]
    lane2 = iota((128, 128), 1)
    edge = jnp.where(
        lane2 == 0,
        pres[:, 0:128],
        jnp.where(
            lane2 == 1,
            pltpu.roll(perm[:, 0:128], 1, 1),
            jnp.where(lane2 == 127, pres[:, 384:512], pltpu.roll(perm[:, 384:512], 127, 1)),
        ),
    )
    edge = edge.T
    col_send[0] = edge[0:8, :]
    col_send[1] = edge[120:128, :]
    hcopies = [
        remote(row_send.at[0], row_recv.at[1], hss.at[0], hrs.at[0], seg_down),
        remote(row_send.at[1], row_recv.at[0], hss.at[1], hrs.at[1], seg_up),
        remote(col_send.at[0], col_recv.at[1], hss.at[2], hrs.at[2], dev_down),
        remote(col_send.at[1], col_recv.at[0], hss.at[3], hrs.at[3], dev_up),
    ]
    for copy in hcopies:
        copy.start()

    cell = cell_r[...]
    cell_lane, cell_block = cell & 127, cell >> 7

    def look(r, found):
        lines = pres[pl.ds(pl.multiple_of(8 * r, 8), 8), :]
        for i in range(8):
            for b in range(4):
                line = jnp.broadcast_to(lines[i : i + 1, 128 * b : 128 * (b + 1)], (8, 128))
                picked = jnp.take_along_axis(line, cell_lane, axis=1)
                found = jnp.where(cell_block == 32 * r + (4 * i + b), picked, found)
        return found

    node_p[...] = lax.fori_loop(0, 16, look, jnp.zeros((8, 128), F32))

    for i in COLUMN_ORDER:
        p = lax.rem(pos + i, NP)
        remote(csend.at[p], crecv.at[p], css.at[i], crs.at[p], column(p)).wait_recv()
    lane32, sub32 = iota((32, 128), 1), iota((32, 128), 0)
    in_turn = ((lane32 & 15) >> 2) == (sub32 >> 3)
    codes = crecv[0]
    for p in range(1, NP):
        codes = jnp.where((iota((8, 128), 1) >> 4) == p, crecv[p], codes)
    xcopies = []
    for h in range(2):
        code = jnp.broadcast_to(codes[h : h + 1, :], (32, 128)).astype(I32)
        scale = jnp.exp2((code >> 3).astype(F32) - (128.0 + 15.0))
        match = ((code & 7) == (sub32 & 7)) & in_turn
        owner[h] = jnp.where(match, 1.0, 0.0).astype(BF16)
        weight = jnp.where(match, scale, 0.0).astype(BF16)
        for i in COLUMN_ORDER:
            p = lax.rem(pos + i, NP)
            remote(zsend.at[h, p], zrecv.at[h, p], zss.at[h, i], zrs.at[h, p], column(p)).wait_recv()
        high, low = split2(zrecv[h].reshape(HALF, 384).astype(I32).astype(F32))
        xsend[4 * h : 4 * (h + 1)] = (dot_nn(weight, high) + dot_nn(weight, low)).reshape(4, 8, 384)
        for i in range(4 * h, min(4 * h + 4, NZ - 1)):
            there, back = row(lax.rem(z + FAR[i], NZ)), FAR.index((NZ - FAR[i]) % NZ)
            xcopies.append(remote(xsend.at[i], xrecv.at[back], xss.at[i], xrs.at[back], there))
            xcopies[-1].start()

    for i in range(4):
        hcopies[i].wait_recv()
    zero_row = jnp.zeros((1, 128), F32)
    above, below = [], []
    for half in range(2):
        for b in range(4):
            above.append(jnp.where(seg > 0, row_recv[0, 4 * half + b : 4 * half + b + 1, :], zero_row))
            below.append(jnp.where(seg < n_seg - 1, row_recv[1, 4 * half + b : 4 * half + b + 1, :], zero_row))
    pres_above, perm_above = jnp.concatenate(above[:4], axis=1), jnp.concatenate(above[4:], axis=1)
    pres_below, perm_below = jnp.concatenate(below[:4], axis=1), jnp.concatenate(below[4:], axis=1)
    sides = jnp.concatenate(
        [
            jnp.where(me > 0, col_recv[0], 0.0),
            jnp.where(me < n_dev - 1, col_recv[1], 0.0),
            jnp.zeros((112, 128), F32),
        ],
        axis=0,
    ).T
    lane8 = iota((8, 512), 1)

    def edge_term(p, k, p2, k2):
        return (2.0 * k * k2 / (k + k2)) * (p - p2)

    for r in range(16):
        rows = slice(8 * r, 8 * (r + 1))
        p, k = pres[rows, :], perm[rows, :]
        if r == 0:
            pu = jnp.concatenate([pres_above, pres[0:7, :]], axis=0)
            ku = jnp.concatenate([perm_above, perm[0:7, :]], axis=0)
        else:
            pu, ku = pres[8 * r - 1 : 8 * r + 7, :], perm[8 * r - 1 : 8 * r + 7, :]
        if r == 15:
            pd = jnp.concatenate([pres[121:128, :], pres_below], axis=0)
            kd = jnp.concatenate([perm[121:128, :], perm_below], axis=0)
        else:
            pd, kd = pres[8 * r + 1 : 8 * r + 9, :], perm[8 * r + 1 : 8 * r + 9, :]
        side = sides[rows, :]
        pl_, kl_ = side[:, 7:8], side[:, 6:7]
        pr_, kr_ = side[:, 8:9], side[:, 9:10]
        pleft = jnp.where(lane8 == 0, pl_, pltpu.roll(p, 1, 1))
        kleft = jnp.where(lane8 == 0, kl_, pltpu.roll(k, 1, 1))
        pright = jnp.where(lane8 == 511, pr_, pltpu.roll(p, 511, 1))
        kright = jnp.where(lane8 == 511, kr_, pltpu.roll(k, 511, 1))
        total = COMPRESS * (p - prev[rows, :])
        total = total + edge_term(p, k, pd, kd) + edge_term(p, k, pu, ku)
        total = total + edge_term(p, k, pright, kright) + edge_term(p, k, pleft, kleft)
        flow_o[rows, :] = total

    mortar_sum = xsend[NZ - 1]
    for i in range(NZ - 2, -1, -1):
        remote(xsend.at[i], xrecv.at[i], xss.at[i], xrs.at[i], row(lax.rem(z + FAR[i], NZ))).wait_recv()
        mortar_sum = mortar_sum + xrecv[i]
    jump = [uplus_r[c] - mortar_sum[:, 128 * c : 128 * (c + 1)] for c in range(3)]
    normal_part = PENALTY * jump[0]
    stress = CONFINING - node_p[...] - normal_part
    softplus = jnp.maximum(stress, 0.0) + jnp.log1p(jnp.exp(-jnp.abs(stress)))
    factor = FRICTION * softplus / jnp.sqrt(jump[1] * jump[1] + jump[2] * jump[2] + 1.0)
    state = state_r[...]
    sliding = [normal_part, jump[1] * factor, jump[2] * factor]
    traction = [
        jnp.where(state == 0, PENALTY * jump[c], jnp.where(state == 1, sliding[c], 0.0)) for c in range(3)
    ]
    tsend[...] = jnp.concatenate(traction + [jnp.zeros((8, 128), F32)], axis=0).astype(BF16)
    tcopies = []
    for i in range(NZ - 1):
        there, back = row(lax.rem(z + FAR[i], NZ)), FAR.index((NZ - FAR[i]) % NZ)
        tcopies.append(remote(tsend, trecv.at[back], tss.at[i], trs.at[back], there))
        tcopies[-1].start()
    trecv[NZ - 1] = tsend[...]
    for c in range(3):
        faces_o[c] = traction[c]

    rcopies = []
    for h in (1, 0):
        for i in range(min(4 * h + 3, NZ - 2), 4 * h - 1, -1):
            remote(tsend, trecv.at[i], tss.at[i], trs.at[i], row(lax.rem(z + FAR[i], NZ))).wait_recv()
        got = trecv[4 * h : 4 * (h + 1)].astype(F32)
        table = jnp.concatenate([got[:, 8 * c : 8 * (c + 1), :].reshape(32, 128) for c in range(3)], axis=1)
        rsend[h] = dot_tn(owner[h], table.astype(BF16)).astype(BF16).reshape(NP, 16, 384)
        for i in COLUMN_ORDER:
            p = lax.rem(pos + i, NP)
            rcopies.append(remote(rsend.at[h, p], rrecv.at[h, pos], rss.at[h, i], rrs.at[h, pos], column(p)))
            rcopies[-1].start()
        rrecv[h, pos] = rsend[h, pos]
    for copy in ccopies + zcopies + hcopies + xcopies + tcopies + rcopies:
        copy.wait_send()
    replies = jnp.zeros((64, 384), F32)
    for h in (1, 0):
        for i in COLUMN_ORDER:
            p = lax.rem(pos + i, NP)
            remote(rsend.at[h, p], rrecv.at[h, p], rss.at[h, i], rrs.at[h, p], column(p)).wait_recv()
        replies = replies + dot_nn(slots_t[:, HALF * h : HALF * (h + 1)], rrecv[h].reshape(HALF, 384))

    patch = iota((8, 128), 0)
    total = jnp.zeros((32, 128), F32)
    for q in range(0, 64, 2):
        left = []
        for k in range(2):
            mine = patch == source_s[q + k]
            rows = [
                jnp.where(mine, jnp.broadcast_to(replies[q + k : q + k + 1, 128 * c : 128 * (c + 1)], (8, 128)), 0.0)
                for c in range(3)
            ]
            left.append(jnp.concatenate(rows + [jnp.zeros((8, 128), F32)], axis=0).astype(BF16))
        total = total + dot_nn(jnp.concatenate(left, axis=1), mort[q : q + 2].reshape(256, 128))
    for c in range(3):
        faces_o[3 + c] = -total[8 * c : 8 * (c + 1), :]


def store_kernel(faces, flow, flow_o, traction_o, force_o, osem):
    stores = [
        pltpu.make_async_copy(faces.at[pl.ds(0, 3)], traction_o, osem.at[0]),
        pltpu.make_async_copy(faces.at[pl.ds(3, 3)], force_o, osem.at[1]),
        pltpu.make_async_copy(flow, flow_o, osem.at[2]),
    ]
    for copy in stores:
        copy.start()
    for copy in stores:
        copy.wait()


def on_device(
    pressure, pressure_prev, permeability, u_plus, u_minus, node_state, node_cell,
    pair_source, pair_dest, pair_target, mortar,
):
    hbm, vmem = (pl.BlockSpec(memory_space=s) for s in (pltpu.HBM, pltpu.VMEM))
    dma = pltpu.SemaphoreType.DMA
    shape = jax.ShapeDtypeStruct
    faces, flow = pl.pallas_call(
        exchange_kernel,
        out_shape=(shape((6, 8, 128), F32), shape((128, 512), F32)),
        in_specs=[hbm] * 11,
        out_specs=(vmem, vmem),
        scratch_shapes=[
            pltpu.VMEM((128, 512), F32),
            pltpu.VMEM((128, 512), F32),
            pltpu.VMEM((128, 512), F32),
            pltpu.VMEM((64, 128, 128), BF16),
            pltpu.VMEM((64, 384), F32),
            pltpu.VMEM((64, 256), BF16),
            pltpu.VMEM((2, 32, HALF), BF16),
            pltpu.VMEM((2, NP, 16, 384), I16),
            pltpu.VMEM((2, NP, 16, 384), I16),
            pltpu.VMEM((NP, 8, 128), F32),
            pltpu.VMEM((NP, 8, 128), F32),
            pltpu.VMEM((NZ, 8, 384), F32),
            pltpu.VMEM((NZ, 8, 384), F32),
            pltpu.VMEM((32, 128), BF16),
            pltpu.VMEM((NZ, 32, 128), BF16),
            pltpu.VMEM((2, NP, 16, 384), BF16),
            pltpu.VMEM((2, NP, 16, 384), BF16),
            pltpu.VMEM((2, 8, 128), F32),
            pltpu.VMEM((2, 8, 128), F32),
            pltpu.VMEM((2, 8, 128), F32),
            pltpu.VMEM((2, 8, 128), F32),
            pltpu.VMEM((8, 128), F32),
            pltpu.VMEM((3, 8, 128), F32),
            pltpu.VMEM((3, 8, 128), BF16),
            pltpu.VMEM((8, 128), I32),
            pltpu.VMEM((8, 128), I32),
            pltpu.VMEM((64,), I32),
            pltpu.VMEM((64,), I32),
            pltpu.SMEM((64,), I32),
            pltpu.VMEM((2, 8, 8, 128), F32),
            dma((4,)), dma((8,)), dma((6,)),
            dma((2, 8)), dma((2, 8)), dma((8,)), dma((8,)), dma((8,)), dma((8,)),
            dma((8,)), dma((8,)), dma((2, 8)), dma((2, 8)), dma((4,)), dma((4,)),
        ],
        compiler_params=pltpu.CompilerParams(
            collective_id=0, has_side_effects=True, vmem_limit_bytes=48 * 1024 * 1024
        ),
        name="exchange",
    )(
        *(
            pltpu.with_memory_space_constraint(a, pltpu.HBM)
            for a in (
                pressure, pressure_prev, permeability, u_plus.transpose(1, 0, 2), u_minus.transpose(1, 0, 2),
                node_state, node_cell, pair_dest.reshape(64), pair_target, pair_source, mortar,
            )
        )
    )
    flow, traction, force = pl.pallas_call(
        store_kernel,
        out_shape=(shape((128, 512), F32), shape((3, 8, 128), F32), shape((3, 8, 128), F32)),
        in_specs=[vmem, vmem],
        out_specs=(hbm, hbm, hbm),
        scratch_shapes=[dma((3,))],
        compiler_params=pltpu.CompilerParams(vmem_limit_bytes=48 * 1024 * 1024),
        name="store",
    )(faces, flow)
    return flow, traction.transpose(1, 0, 2), force.transpose(1, 0, 2)


def solution(mesh):
    both = ("seg", "dev")
    cells, patches = P("seg", "dev"), P(both, None, None)
    placed = (
        cells, cells, cells, patches, patches, P(both, None), P(both, None), P(both), P(both, None), P(both), patches,
    )
    return jax.shard_map(
        on_device, mesh=mesh, in_specs=placed, out_specs=(cells, patches, patches), check_vma=False
    )
```

```python
import jax
import jax.numpy as jnp
from jax import lax
from jax.experimental import pallas as pl
from jax.experimental.pallas import tpu as pltpu
from jax.sharding import PartitionSpec as P

CAP = 4
COMPRESS = 0.5
PENALTY = 1.5
FRICTION = 0.6
CONFINING = 1.0

NP = 8
NZ = 8
FAR = (4, 3, 5, 2, 6, 1, 7, 0)
COLUMN_ORDER = (4, 5, 3, 2, 6, 1, 7)
HALF = NP * 16
F32 = jnp.float32
BF16 = jnp.bfloat16
I32 = jnp.int32
I16 = jnp.int16
MESH = pl.DeviceIdType.MESH


def iota(shape, dim):
    return lax.broadcasted_iota(I32, shape, dim)


def split2(value):
    high = value.astype(BF16)
    return high, (value - high.astype(F32)).astype(BF16)


def dot_nn(a, b):
    return lax.dot_general(a, b, (((1,), (0,)), ((), ())), preferred_element_type=F32)


def dot_nt(a, b):
    return lax.dot_general(a, b, (((1,), (1,)), ((), ())), preferred_element_type=F32)


def dot_tn(a, b):
    return lax.dot_general(a, b, (((0,), (0,)), ((), ())), preferred_element_type=F32)


def remote(src, dst, send, recv, device):
    return pltpu.make_async_remote_copy(
        src_ref=src, dst_ref=dst, send_sem=send, recv_sem=recv, device_id=device, device_id_type=MESH
    )


def exchange_kernel(
    pressure_h, prev_h, perm_h, uplus_h, uminus_h, state_h, cell_h, dest_h, target_h, source_h, mortar_h,
    faces_o, flow_o,
    pres, prev, perm, mort, proj, slots_t, owner, zsend, zrecv, csend, crecv, xsend, xrecv,
    tsend, trecv, rsend, rrecv, row_send, row_recv, col_send, col_recv, node_p,
    uplus_r, uminus_r, state_r, cell_r, dest_r, target_r, source_s, by_patch,
    fsem, msem, lsem, zss, zrs, css, crs, xss, xrs, tss, trs, rss, rrs, hss, hrs,
):
    seg = lax.axis_index("seg")
    me = lax.axis_index("dev")
    n_seg = lax.axis_size("seg")
    n_dev = lax.axis_size("dev")
    z, pos = me // NP, lax.rem(me, NP)

    def column(p):
        return {"dev": z * NP + p}

    def row(zz):
        return {"dev": zz * NP + pos}

    seg_up, seg_down = {"seg": lax.rem(seg + 1, n_seg)}, {"seg": lax.rem(seg + n_seg - 1, n_seg)}
    dev_up, dev_down = {"dev": lax.rem(me + 1, n_dev)}, {"dev": lax.rem(me + n_dev - 1, n_dev)}

    barrier = pltpu.get_barrier_semaphore()
    neighbours = [row(lax.rem(z + i, NZ)) for i in FAR[:7]]
    neighbours += [column(lax.rem(pos + i, NP)) for i in COLUMN_ORDER]
    neighbours += [seg_up, seg_down, dev_up, dev_down]
    for device in neighbours:
        pl.semaphore_signal(barrier, inc=1, device_id=device, device_id_type=MESH)

    def fetch(pairs, sems):
        copies = [pltpu.make_async_copy(a, b, sems.at[i]) for i, (a, b) in enumerate(pairs)]
        for copy in copies:
            copy.start()
        return copies

    first = fetch(((dest_h, dest_r), (target_h, target_r), (source_h, source_s), (uminus_h, uminus_r)), fsem)
    mcopies = fetch([(mortar_h.at[pl.ds(8 * g, 8)], mort.at[pl.ds(8 * g, 8)]) for g in range(8)], msem)
    for copy in first:
        copy.wait()
    by_patch[...] = jnp.zeros_like(by_patch)
    for b in range(8):
        for c in range(3):
            by_patch[0, b, c : c + 1, :] = uminus_r[c].astype(F32)[b : b + 1, :]
            by_patch[1, b, 4 + c : 5 + c, :] = uminus_r[c].astype(F32)[b : b + 1, :]

    lane, sub = iota((64, 128), 1), iota((64, 128), 0)
    diagonal = lane == sub

    def as_column(ref):
        wide = jnp.concatenate([ref[...].reshape(1, 64), jnp.full((1, 64), -1, I32)], axis=1)
        wide = jnp.broadcast_to(wide, (64, 128))
        return wide, jnp.sum(jnp.where(diagonal, wide, 0), axis=1, keepdims=True)

    dest_row, dest = as_column(dest_r)
    _, target = as_column(target_r)
    rank = jnp.sum(jnp.where((dest_row == dest) & (lane < sub), 1, 0), axis=1, keepdims=True)
    distance = ((dest >> 3) + NZ - z) & (NZ - 1)
    turn = jnp.zeros((64, 1), I32)
    for i in range(NZ):
        turn = jnp.where(distance == FAR[i], i, turn)
    slot = (turn >> 2) * HALF + (dest & (NP - 1)) * 16 + (turn & 3) * CAP + rank
    for h in range(2):
        slots_t[:, 128 * h : 128 * (h + 1)] = jnp.where(slot == lane + 128 * h, 1.0, 0.0).astype(BF16)
    for copy in mcopies:
        copy.wait()
    lcopies = fetch(
        (
            (pressure_h, pres), (cell_h, cell_r), (perm_h, perm), (prev_h, prev),
            (uplus_h, uplus_r), (state_h, state_r),
        ),
        lsem,
    )

    for g in range(8):
        lines = [[], [], []]
        for j in range(0, 8, 2):
            q = 8 * g + j
            left = (by_patch[0, source_s[q]] + by_patch[1, source_s[q + 1]]).astype(BF16)
            value = dot_nt(left, mort[q : q + 2].reshape(256, 128))
            for c in range(3):
                lines[c] += [value[c : c + 1, 0:128], value[4 + c : 5 + c, 128:256]]
        for c in range(3):
            proj[8 * g : 8 * (g + 1), 128 * c : 128 * (c + 1)] = jnp.concatenate(lines[c], axis=0)
    size = jnp.max(jnp.abs(proj[...]), axis=1, keepdims=True)
    power = jnp.floor(jnp.log2(jnp.maximum(size, 1e-30))) + 1.0
    whole = jnp.clip(jnp.round(proj[...] * jnp.exp2(15.0 - power)), -32767.0, 32767.0)
    label = target.astype(F32) + 8.0 * (power + 128.0)
    for p in range(NP):
        for h in range(2):
            spot = slot == (lane & 15) + (h * HALF + 16 * p)
            csend[p, h : h + 1, :] = jnp.sum(jnp.where(spot, label, 0.0), axis=0, keepdims=True)
    high, low = split2(whole)

    def place(h):
        hit = slots_t[:, HALF * h : HALF * (h + 1)]
        zsend[h] = (dot_tn(hit, high) + dot_tn(hit, low)).astype(I32).astype(I16).reshape(NP, 16, 384)

    place(0)
    pl.semaphore_wait(barrier, len(neighbours))

    ccopies, zcopies = [], []
    for i in COLUMN_ORDER:
        p = lax.rem(pos + i, NP)
        ccopies.append(remote(csend.at[p, pl.ds(0, 2)], crecv.at[pos, pl.ds(0, 2)], css.at[i], crs.at[pos], column(p)))
        zcopies.append(remote(zsend.at[0, p], zrecv.at[0, pos], zss.at[0, i], zrs.at[0, pos], column(p)))
        ccopies[-1].start()
        zcopies[-1].start()
    place(1)
    for i in COLUMN_ORDER:
        p = lax.rem(pos + i, NP)
        zcopies.append(remote(zsend.at[1, p], zrecv.at[1, pos], zss.at[1, i], zrs.at[1, pos], column(p)))
        zcopies[-1].start()
    crecv[pos] = csend[pos]
    for h in range(2):
        zrecv[h, pos] = zsend[h, pos]

    for copy in lcopies:
        copy.wait()
    for b in range(4):
        cut = slice(128 * b, 128 * (b + 1))
        row_send[0, b : b + 1, :] = pres[0:1, cut]
        row_send[0, 4 + b : 5 + b, :] = perm[0:1, cut]
        row_send[1, b : b + 1, :] = pres[127:128, cut]
        row_send[1, 4 + b : 5 + b, :] = perm[127:128, cut]
    lane2 = iota((128, 128), 1)
    edge = jnp.where(
        lane2 == 0,
        pres[:, 0:128],
        jnp.where(
            lane2 == 1,
            pltpu.roll(perm[:, 0:128], 1, 1),
            jnp.where(lane2 == 127, pres[:, 384:512], pltpu.roll(perm[:, 384:512], 127, 1)),
        ),
    )
    edge = edge.T
    col_send[0] = edge[0:8, :]
    col_send[1] = edge[120:128, :]
    hcopies = [
        remote(row_send.at[0], row_recv.at[1], hss.at[0], hrs.at[0], seg_down),
        remote(row_send.at[1], row_recv.at[0], hss.at[1], hrs.at[1], seg_up),
        remote(col_send.at[0], col_recv.at[1], hss.at[2], hrs.at[2], dev_down),
        remote(col_send.at[1], col_recv.at[0], hss.at[3], hrs.at[3], dev_up),
    ]
    for copy in hcopies:
        copy.start()

    cell = cell_r[...]
    cell_lane, cell_block = cell & 127, cell >> 7

    def look(r, found):
        lines = pres[pl.ds(pl.multiple_of(8 * r, 8), 8), :]
        for i in range(8):
            for b in range(4):
                line = jnp.broadcast_to(lines[i : i + 1, 128 * b : 128 * (b + 1)], (8, 128))
                picked = jnp.take_along_axis(line, cell_lane, axis=1)
                found = jnp.where(cell_block == 32 * r + (4 * i + b), picked, found)
        return found

    node_p[...] = lax.fori_loop(0, 16, look, jnp.zeros((8, 128), F32))

    for i in COLUMN_ORDER:
        p = lax.rem(pos + i, NP)
        remote(csend.at[p, pl.ds(0, 2)], crecv.at[p, pl.ds(0, 2)], css.at[i], crs.at[p], column(p)).wait_recv()
    lane32, sub32 = iota((32, 128), 1), iota((32, 128), 0)
    in_turn = ((lane32 & 15) >> 2) == (sub32 >> 3)
    codes = crecv[0]
    for p in range(1, NP):
        codes = jnp.where((iota((8, 128), 1) >> 4) == p, crecv[p], codes)
    xcopies = []
    for h in range(2):
        code = jnp.broadcast_to(codes[h : h + 1, :], (32, 128)).astype(I32)
        scale = jnp.exp2((code >> 3).astype(F32) - (128.0 + 15.0))
        match = ((code & 7) == (sub32 & 7)) & in_turn
        owner[h] = jnp.where(match, 1.0, 0.0).astype(BF16)
        weight = jnp.where(match, scale, 0.0).astype(BF16)
        for i in COLUMN_ORDER:
            p = lax.rem(pos + i, NP)
            remote(zsend.at[h, p], zrecv.at[h, p], zss.at[h, i], zrs.at[h, p], column(p)).wait_recv()
        high, low = split2(zrecv[h].reshape(HALF, 384).astype(I32).astype(F32))
        xsend[4 * h : 4 * (h + 1)] = (dot_nn(weight, high) + dot_nn(weight, low)).reshape(4, 8, 384)
        for i in range(4 * h, min(4 * h + 4, NZ - 1)):
            there, back = row(lax.rem(z + FAR[i], NZ)), FAR.index((NZ - FAR[i]) % NZ)
            xcopies.append(remote(xsend.at[i], xrecv.at[back], xss.at[i], xrs.at[back], there))
            xcopies[-1].start()

    for i in range(4):
        hcopies[i].wait_recv()
    zero_row = jnp.zeros((1, 128), F32)
    above, below = [], []
    for half in range(2):
        for b in range(4):
            above.append(jnp.where(seg > 0, row_recv[0, 4 * half + b : 4 * half + b + 1, :], zero_row))
            below.append(jnp.where(seg < n_seg - 1, row_recv[1, 4 * half + b : 4 * half + b + 1, :], zero_row))
    pres_above, perm_above = jnp.concatenate(above[:4], axis=1), jnp.concatenate(above[4:], axis=1)
    pres_below, perm_below = jnp.concatenate(below[:4], axis=1), jnp.concatenate(below[4:], axis=1)
    sides = jnp.concatenate(
        [
            jnp.where(me > 0, col_recv[0], 0.0),
            jnp.where(me < n_dev - 1, col_recv[1], 0.0),
            jnp.zeros((112, 128), F32),
        ],
        axis=0,
    ).T
    lane8 = iota((8, 512), 1)

    def edge_term(p, k, p2, k2):
        return (2.0 * k * k2 / (k + k2)) * (p - p2)

    for r in range(16):
        rows = slice(8 * r, 8 * (r + 1))
        p, k = pres[rows, :], perm[rows, :]
        if r == 0:
            pu = jnp.concatenate([pres_above, pres[0:7, :]], axis=0)
            ku = jnp.concatenate([perm_above, perm[0:7, :]], axis=0)
        else:
            pu, ku = pres[8 * r - 1 : 8 * r + 7, :], perm[8 * r - 1 : 8 * r + 7, :]
        if r == 15:
            pd = jnp.concatenate([pres[121:128, :], pres_below], axis=0)
            kd = jnp.concatenate([perm[121:128, :], perm_below], axis=0)
        else:
            pd, kd = pres[8 * r + 1 : 8 * r + 9, :], perm[8 * r + 1 : 8 * r + 9, :]
        side = sides[rows, :]
        pl_, kl_ = side[:, 7:8], side[:, 6:7]
        pr_, kr_ = side[:, 8:9], side[:, 9:10]
        pleft = jnp.where(lane8 == 0, pl_, pltpu.roll(p, 1, 1))
        kleft = jnp.where(lane8 == 0, kl_, pltpu.roll(k, 1, 1))
        pright = jnp.where(lane8 == 511, pr_, pltpu.roll(p, 511, 1))
        kright = jnp.where(lane8 == 511, kr_, pltpu.roll(k, 511, 1))
        total = COMPRESS * (p - prev[rows, :])
        total = total + edge_term(p, k, pd, kd) + edge_term(p, k, pu, ku)
        total = total + edge_term(p, k, pright, kright) + edge_term(p, k, pleft, kleft)
        flow_o[rows, :] = total

    mortar_sum = xsend[NZ - 1]
    for i in range(NZ - 2, -1, -1):
        remote(xsend.at[i], xrecv.at[i], xss.at[i], xrs.at[i], row(lax.rem(z + FAR[i], NZ))).wait_recv()
        mortar_sum = mortar_sum + xrecv[i]
    jump = [uplus_r[c] - mortar_sum[:, 128 * c : 128 * (c + 1)] for c in range(3)]
    normal_part = PENALTY * jump[0]
    stress = CONFINING - node_p[...] - normal_part
    softplus = jnp.maximum(stress, 0.0) + jnp.log1p(jnp.exp(-jnp.abs(stress)))
    factor = FRICTION * softplus / jnp.sqrt(jump[1] * jump[1] + jump[2] * jump[2] + 1.0)
    state = state_r[...]
    sliding = [normal_part, jump[1] * factor, jump[2] * factor]
    traction = [
        jnp.where(state == 0, PENALTY * jump[c], jnp.where(state == 1, sliding[c], 0.0)) for c in range(3)
    ]
    tsend[...] = jnp.concatenate(traction + [jnp.zeros((8, 128), F32)], axis=0).astype(BF16)
    tcopies = []
    for i in range(NZ - 1):
        there, back = row(lax.rem(z + FAR[i], NZ)), FAR.index((NZ - FAR[i]) % NZ)
        tcopies.append(remote(tsend, trecv.at[back], tss.at[i], trs.at[back], there))
        tcopies[-1].start()
    trecv[NZ - 1] = tsend[...]
    for c in range(3):
        faces_o[c] = traction[c]

    rcopies = []
    for h in (1, 0):
        for i in range(min(4 * h + 3, NZ - 2), 4 * h - 1, -1):
            remote(tsend, trecv.at[i], tss.at[i], trs.at[i], row(lax.rem(z + FAR[i], NZ))).wait_recv()
        got = trecv[4 * h : 4 * (h + 1)].astype(F32)
        table = jnp.concatenate([got[:, 8 * c : 8 * (c + 1), :].reshape(32, 128) for c in range(3)], axis=1)
        rsend[h] = dot_tn(owner[h], table.astype(BF16)).astype(BF16).reshape(NP, 16, 384)
        for i in COLUMN_ORDER:
            p = lax.rem(pos + i, NP)
            rcopies.append(remote(rsend.at[h, p], rrecv.at[h, pos], rss.at[h, i], rrs.at[h, pos], column(p)))
            rcopies[-1].start()
        rrecv[h, pos] = rsend[h, pos]
    for copy in ccopies + zcopies + hcopies + xcopies + tcopies + rcopies:
        copy.wait_send()
    replies = jnp.zeros((64, 384), F32)
    for h in (1, 0):
        for i in COLUMN_ORDER:
            p = lax.rem(pos + i, NP)
            remote(rsend.at[h, p], rrecv.at[h, p], rss.at[h, i], rrs.at[h, p], column(p)).wait_recv()
        replies = replies + dot_nn(slots_t[:, HALF * h : HALF * (h + 1)], rrecv[h].reshape(HALF, 384))

    patch = iota((8, 128), 0)
    total = jnp.zeros((32, 128), F32)
    for q in range(0, 64, 2):
        left = []
        for k in range(2):
            mine = patch == source_s[q + k]
            rows = [
                jnp.where(mine, jnp.broadcast_to(replies[q + k : q + k + 1, 128 * c : 128 * (c + 1)], (8, 128)), 0.0)
                for c in range(3)
            ]
            left.append(jnp.concatenate(rows + [jnp.zeros((8, 128), F32)], axis=0).astype(BF16))
        total = total + dot_nn(jnp.concatenate(left, axis=1), mort[q : q + 2].reshape(256, 128))
    for c in range(3):
        faces_o[3 + c] = -total[8 * c : 8 * (c + 1), :]


def store_kernel(faces, flow, flow_o, traction_o, force_o, osem):
    stores = [
        pltpu.make_async_copy(faces.at[pl.ds(0, 3)], traction_o, osem.at[0]),
        pltpu.make_async_copy(faces.at[pl.ds(3, 3)], force_o, osem.at[1]),
        pltpu.make_async_copy(flow, flow_o, osem.at[2]),
    ]
    for copy in stores:
        copy.start()
    for copy in stores:
        copy.wait()


def on_device(
    pressure, pressure_prev, permeability, u_plus, u_minus, node_state, node_cell,
    pair_source, pair_dest, pair_target, mortar,
):
    hbm, vmem = (pl.BlockSpec(memory_space=s) for s in (pltpu.HBM, pltpu.VMEM))
    dma = pltpu.SemaphoreType.DMA
    shape = jax.ShapeDtypeStruct
    faces, flow = pl.pallas_call(
        exchange_kernel,
        out_shape=(shape((6, 8, 128), F32), shape((128, 512), F32)),
        in_specs=[hbm] * 11,
        out_specs=(vmem, vmem),
        scratch_shapes=[
            pltpu.VMEM((128, 512), F32),
            pltpu.VMEM((128, 512), F32),
            pltpu.VMEM((128, 512), F32),
            pltpu.VMEM((64, 128, 128), BF16),
            pltpu.VMEM((64, 384), F32),
            pltpu.VMEM((64, 256), BF16),
            pltpu.VMEM((2, 32, HALF), BF16),
            pltpu.VMEM((2, NP, 16, 384), I16),
            pltpu.VMEM((2, NP, 16, 384), I16),
            pltpu.VMEM((NP, 8, 128), F32),
            pltpu.VMEM((NP, 8, 128), F32),
            pltpu.VMEM((NZ, 8, 384), F32),
            pltpu.VMEM((NZ, 8, 384), F32),
            pltpu.VMEM((32, 128), BF16),
            pltpu.VMEM((NZ, 32, 128), BF16),
            pltpu.VMEM((2, NP, 16, 384), BF16),
            pltpu.VMEM((2, NP, 16, 384), BF16),
            pltpu.VMEM((2, 8, 128), F32),
            pltpu.VMEM((2, 8, 128), F32),
            pltpu.VMEM((2, 8, 128), F32),
            pltpu.VMEM((2, 8, 128), F32),
            pltpu.VMEM((8, 128), F32),
            pltpu.VMEM((3, 8, 128), F32),
            pltpu.VMEM((3, 8, 128), BF16),
            pltpu.VMEM((8, 128), I32),
            pltpu.VMEM((8, 128), I32),
            pltpu.VMEM((64,), I32),
            pltpu.VMEM((64,), I32),
            pltpu.SMEM((64,), I32),
            pltpu.VMEM((2, 8, 8, 128), F32),
            dma((4,)), dma((8,)), dma((6,)),
            dma((2, 8)), dma((2, 8)), dma((8,)), dma((8,)), dma((8,)), dma((8,)),
            dma((8,)), dma((8,)), dma((2, 8)), dma((2, 8)), dma((4,)), dma((4,)),
        ],
        compiler_params=pltpu.CompilerParams(
            collective_id=0, has_side_effects=True, vmem_limit_bytes=48 * 1024 * 1024
        ),
        name="exchange",
    )(
        *(
            pltpu.with_memory_space_constraint(a, pltpu.HBM)
            for a in (
                pressure, pressure_prev, permeability, u_plus.transpose(1, 0, 2), u_minus.transpose(1, 0, 2),
                node_state, node_cell, pair_dest.reshape(64), pair_target, pair_source, mortar,
            )
        )
    )
    flow, traction, force = pl.pallas_call(
        store_kernel,
        out_shape=(shape((128, 512), F32), shape((3, 8, 128), F32), shape((3, 8, 128), F32)),
        in_specs=[vmem, vmem],
        out_specs=(hbm, hbm, hbm),
        scratch_shapes=[dma((3,))],
        compiler_params=pltpu.CompilerParams(vmem_limit_bytes=48 * 1024 * 1024),
        name="store",
    )(faces, flow)
    return flow, traction.transpose(1, 0, 2), force.transpose(1, 0, 2)


def solution(mesh):
    both = ("seg", "dev")
    cells, patches = P("seg", "dev"), P(both, None, None)
    placed = (
        cells, cells, cells, patches, patches, P(both, None), P(both, None), P(both), P(both, None), P(both), patches,
    )
    return jax.shard_map(
        on_device, mesh=mesh, in_specs=placed, out_specs=(cells, patches, patches), check_vma=False
    )
```

```python
import jax
import jax.numpy as jnp
from jax import lax
from jax.experimental import pallas as pl
from jax.experimental.pallas import tpu as pltpu
from jax.sharding import PartitionSpec as P

CAP = 4
COMPRESS = 0.5
PENALTY = 1.5
FRICTION = 0.6
CONFINING = 1.0

NP = 8
NZ = 8
FAR = (4, 3, 5, 2, 6, 1, 7, 0)
COLUMN_ORDER = (4, 5, 3, 2, 6, 1, 7)
HALF = NP * 16
F32 = jnp.float32
BF16 = jnp.bfloat16
I32 = jnp.int32
I16 = jnp.int16
MESH = pl.DeviceIdType.MESH


def iota(shape, dim):
    return lax.broadcasted_iota(I32, shape, dim)


def split2(value):
    high = value.astype(BF16)
    return high, (value - high.astype(F32)).astype(BF16)


def dot_nn(a, b):
    return lax.dot_general(a, b, (((1,), (0,)), ((), ())), preferred_element_type=F32)


def dot_nt(a, b):
    return lax.dot_general(a, b, (((1,), (1,)), ((), ())), preferred_element_type=F32)


def dot_tn(a, b):
    return lax.dot_general(a, b, (((0,), (0,)), ((), ())), preferred_element_type=F32)


def remote(src, dst, send, recv, device):
    return pltpu.make_async_remote_copy(
        src_ref=src, dst_ref=dst, send_sem=send, recv_sem=recv, device_id=device, device_id_type=MESH
    )


def exchange_kernel(
    pressure_h, prev_h, perm_h, uplus_h, uminus_h, state_h, cell_h, dest_h, target_h, source_h, mortar_h,
    faces_o, flow_o,
    pres, prev, perm, mort, proj, slots_t, owner, zsend, zrecv, csend, crecv, xsend, xrecv,
    tsend, trecv, rsend, rrecv, row_send, row_recv, col_send, col_recv, node_p,
    uplus_r, uminus_r, state_r, cell_r, dest_r, target_r, source_s, by_patch,
    fsem, msem, lsem, zss, zrs, css, crs, xss, xrs, tss, trs, rss, rrs, hss, hrs,
):
    seg = lax.axis_index("seg")
    me = lax.axis_index("dev")
    n_seg = lax.axis_size("seg")
    n_dev = lax.axis_size("dev")
    z, pos = me // NP, lax.rem(me, NP)

    def column(p):
        return {"dev": z * NP + p}

    def row(zz):
        return {"dev": zz * NP + pos}

    seg_up, seg_down = {"seg": lax.rem(seg + 1, n_seg)}, {"seg": lax.rem(seg + n_seg - 1, n_seg)}
    dev_up, dev_down = {"dev": lax.rem(me + 1, n_dev)}, {"dev": lax.rem(me + n_dev - 1, n_dev)}

    barrier = pltpu.get_barrier_semaphore()
    neighbours = [row(lax.rem(z + i, NZ)) for i in FAR[:7]]
    neighbours += [column(lax.rem(pos + i, NP)) for i in COLUMN_ORDER]
    neighbours += [seg_up, seg_down, dev_up, dev_down]
    for device in neighbours:
        pl.semaphore_signal(barrier, inc=1, device_id=device, device_id_type=MESH)

    def fetch(pairs, sems):
        copies = [pltpu.make_async_copy(a, b, sems.at[i]) for i, (a, b) in enumerate(pairs)]
        for copy in copies:
            copy.start()
        return copies

    first = fetch(((dest_h, dest_r), (target_h, target_r), (source_h, source_s), (uminus_h, uminus_r)), fsem)
    mcopies = fetch([(mortar_h.at[pl.ds(8 * g, 8)], mort.at[pl.ds(8 * g, 8)]) for g in range(8)], msem)
    for copy in first:
        copy.wait()
    by_patch[...] = jnp.zeros_like(by_patch)
    for b in range(8):
        for c in range(3):
            by_patch[0, b, c : c + 1, :] = uminus_r[c].astype(F32)[b : b + 1, :]
            by_patch[1, b, 4 + c : 5 + c, :] = uminus_r[c].astype(F32)[b : b + 1, :]

    lane, sub = iota((64, 128), 1), iota((64, 128), 0)
    diagonal = lane == sub

    def as_column(ref):
        wide = jnp.concatenate([ref[...].reshape(1, 64), jnp.full((1, 64), -1, I32)], axis=1)
        wide = jnp.broadcast_to(wide, (64, 128))
        return wide, jnp.sum(jnp.where(diagonal, wide, 0), axis=1, keepdims=True)

    dest_row, dest = as_column(dest_r)
    _, target = as_column(target_r)
    rank = jnp.sum(jnp.where((dest_row == dest) & (lane < sub), 1, 0), axis=1, keepdims=True)
    distance = ((dest >> 3) + NZ - z) & (NZ - 1)
    turn = jnp.zeros((64, 1), I32)
    for i in range(NZ):
        turn = jnp.where(distance == FAR[i], i, turn)
    slot = (turn >> 2) * HALF + (dest & (NP - 1)) * 16 + (turn & 3) * CAP + rank
    for h in range(2):
        slots_t[:, 128 * h : 128 * (h + 1)] = jnp.where(slot == lane + 128 * h, 1.0, 0.0).astype(BF16)
    for copy in mcopies:
        copy.wait()
    lcopies = fetch(
        (
            (pressure_h, pres), (cell_h, cell_r), (perm_h, perm), (prev_h, prev),
            (uplus_h, uplus_r), (state_h, state_r),
        ),
        lsem,
    )

    for g in range(8):
        lines = [[], [], []]
        for j in range(0, 8, 2):
            q = 8 * g + j
            left = (by_patch[0, source_s[q]] + by_patch[1, source_s[q + 1]]).astype(BF16)
            value = dot_nt(left, mort[q : q + 2].reshape(256, 128))
            for c in range(3):
                lines[c] += [value[c : c + 1, 0:128], value[4 + c : 5 + c, 128:256]]
        for c in range(3):
            proj[8 * g : 8 * (g + 1), 128 * c : 128 * (c + 1)] = jnp.concatenate(lines[c], axis=0)
    size = jnp.max(jnp.abs(proj[...]), axis=1, keepdims=True)
    power = jnp.floor(jnp.log2(jnp.maximum(size, 1e-30))) + 1.0
    whole = jnp.clip(jnp.round(proj[...] * jnp.exp2(15.0 - power)), -32767.0, 32767.0)
    label = target.astype(F32) + 8.0 * (power + 128.0)
    for p in range(NP):
        for h in range(2):
            spot = slot == (lane & 15) + (h * HALF + 16 * p)
            csend[p, h : h + 1, :] = jnp.sum(jnp.where(spot, label, 0.0), axis=0, keepdims=True)
    high, low = split2(whole)

    def place(h):
        hit = slots_t[:, HALF * h : HALF * (h + 1)]
        zsend[h] = (dot_tn(hit, high) + dot_tn(hit, low)).astype(I32).astype(I16).reshape(NP, 16, 384)

    place(0)
    pl.semaphore_wait(barrier, len(neighbours))

    ccopies, zcopies = [], []
    for i in COLUMN_ORDER:
        p = lax.rem(pos + i, NP)
        ccopies.append(remote(csend.at[p, pl.ds(0, 2)], crecv.at[pos, pl.ds(0, 2)], css.at[i], crs.at[pos], column(p)))
        zcopies.append(remote(zsend.at[0, p], zrecv.at[0, pos], zss.at[0, i], zrs.at[0, pos], column(p)))
        ccopies[-1].start()
        zcopies[-1].start()
    place(1)
    for i in COLUMN_ORDER:
        p = lax.rem(pos + i, NP)
        zcopies.append(remote(zsend.at[1, p], zrecv.at[1, pos], zss.at[1, i], zrs.at[1, pos], column(p)))
        zcopies[-1].start()
    crecv[pos] = csend[pos]
    for h in range(2):
        zrecv[h, pos] = zsend[h, pos]

    for copy in lcopies:
        copy.wait()
    for b in range(4):
        cut = slice(128 * b, 128 * (b + 1))
        row_send[0, b : b + 1, :] = pres[0:1, cut]
        row_send[0, 4 + b : 5 + b, :] = perm[0:1, cut]
        row_send[1, b : b + 1, :] = pres[127:128, cut]
        row_send[1, 4 + b : 5 + b, :] = perm[127:128, cut]
    lane2 = iota((128, 128), 1)
    edge = jnp.where(
        lane2 == 0,
        pres[:, 0:128],
        jnp.where(
            lane2 == 1,
            pltpu.roll(perm[:, 0:128], 1, 1),
            jnp.where(lane2 == 127, pres[:, 384:512], pltpu.roll(perm[:, 384:512], 127, 1)),
        ),
    )
    edge = edge.T
    col_send[0] = edge[0:8, :]
    col_send[1] = edge[120:128, :]
    hcopies = [
        remote(row_send.at[0], row_recv.at[1], hss.at[0], hrs.at[0], seg_down),
        remote(row_send.at[1], row_recv.at[0], hss.at[1], hrs.at[1], seg_up),
        remote(col_send.at[0], col_recv.at[1], hss.at[2], hrs.at[2], dev_down),
        remote(col_send.at[1], col_recv.at[0], hss.at[3], hrs.at[3], dev_up),
    ]
    for copy in hcopies:
        copy.start()

    cell = cell_r[...]
    cell_lane, cell_block = cell & 127, cell >> 7

    def look(r, found):
        lines = pres[pl.ds(pl.multiple_of(8 * r, 8), 8), :]
        for i in range(8):
            for b in range(4):
                line = jnp.broadcast_to(lines[i : i + 1, 128 * b : 128 * (b + 1)], (8, 128))
                picked = jnp.take_along_axis(line, cell_lane, axis=1)
                found = jnp.where(cell_block == 32 * r + (4 * i + b), picked, found)
        return found

    node_p[...] = lax.fori_loop(0, 16, look, jnp.zeros((8, 128), F32))

    for i in COLUMN_ORDER:
        p = lax.rem(pos + i, NP)
        remote(csend.at[p, pl.ds(0, 2)], crecv.at[p, pl.ds(0, 2)], css.at[i], crs.at[p], column(p)).wait_recv()
    lane32, sub32 = iota((32, 128), 1), iota((32, 128), 0)
    in_turn = ((lane32 & 15) >> 2) == (sub32 >> 3)
    codes = crecv[0]
    for p in range(1, NP):
        codes = jnp.where((iota((8, 128), 1) >> 4) == p, crecv[p], codes)
    xcopies = []
    for h in range(2):
        code = jnp.broadcast_to(codes[h : h + 1, :], (32, 128)).astype(I32)
        scale = jnp.exp2((code >> 3).astype(F32) - (128.0 + 15.0))
        match = ((code & 7) == (sub32 & 7)) & in_turn
        owner[h] = jnp.where(match, 1.0, 0.0).astype(BF16)
        weight = jnp.where(match, scale, 0.0).astype(BF16)
        for i in COLUMN_ORDER:
            p = lax.rem(pos + i, NP)
            remote(zsend.at[h, p], zrecv.at[h, p], zss.at[h, i], zrs.at[h, p], column(p)).wait_recv()
        high, low = split2(zrecv[h].reshape(HALF, 384).astype(I32).astype(F32))
        dense = dot_nn(weight, high) + dot_nn(weight, low)
        size = jnp.max(jnp.abs(dense), axis=1, keepdims=True)
        power = jnp.floor(jnp.log2(jnp.maximum(size, 1e-30))) + 1.0
        whole = jnp.clip(jnp.round(dense * jnp.exp2(15.0 - power)), -32767.0, 32767.0)
        blocks = [whole[:, 128 * c : 128 * (c + 1)].reshape(4, 8, 128) for c in range(3)]
        blocks.append(jnp.broadcast_to(power, (32, 128)).reshape(4, 8, 128))
        xsend[4 * h : 4 * (h + 1)] = jnp.concatenate(blocks, axis=1).astype(I32).astype(I16)
        for i in range(4 * h, min(4 * h + 4, NZ - 1)):
            there, back = row(lax.rem(z + FAR[i], NZ)), FAR.index((NZ - FAR[i]) % NZ)
            xcopies.append(remote(xsend.at[i], xrecv.at[back], xss.at[i], xrs.at[back], there))
            xcopies[-1].start()

    for i in range(4):
        hcopies[i].wait_recv()
    zero_row = jnp.zeros((1, 128), F32)
    above, below = [], []
    for half in range(2):
        for b in range(4):
            above.append(jnp.where(seg > 0, row_recv[0, 4 * half + b : 4 * half + b + 1, :], zero_row))
            below.append(jnp.where(seg < n_seg - 1, row_recv[1, 4 * half + b : 4 * half + b + 1, :], zero_row))
    pres_above, perm_above = jnp.concatenate(above[:4], axis=1), jnp.concatenate(above[4:], axis=1)
    pres_below, perm_below = jnp.concatenate(below[:4], axis=1), jnp.concatenate(below[4:], axis=1)
    sides = jnp.concatenate(
        [
            jnp.where(me > 0, col_recv[0], 0.0),
            jnp.where(me < n_dev - 1, col_recv[1], 0.0),
            jnp.zeros((112, 128), F32),
        ],
        axis=0,
    ).T
    lane8 = iota((8, 512), 1)

    def edge_term(p, k, p2, k2):
        return (2.0 * k * k2 / (k + k2)) * (p - p2)

    for r in range(16):
        rows = slice(8 * r, 8 * (r + 1))
        p, k = pres[rows, :], perm[rows, :]
        if r == 0:
            pu = jnp.concatenate([pres_above, pres[0:7, :]], axis=0)
            ku = jnp.concatenate([perm_above, perm[0:7, :]], axis=0)
        else:
            pu, ku = pres[8 * r - 1 : 8 * r + 7, :], perm[8 * r - 1 : 8 * r + 7, :]
        if r == 15:
            pd = jnp.concatenate([pres[121:128, :], pres_below], axis=0)
            kd = jnp.concatenate([perm[121:128, :], perm_below], axis=0)
        else:
            pd, kd = pres[8 * r + 1 : 8 * r + 9, :], perm[8 * r + 1 : 8 * r + 9, :]
        side = sides[rows, :]
        pl_, kl_ = side[:, 7:8], side[:, 6:7]
        pr_, kr_ = side[:, 8:9], side[:, 9:10]
        pleft = jnp.where(lane8 == 0, pl_, pltpu.roll(p, 1, 1))
        kleft = jnp.where(lane8 == 0, kl_, pltpu.roll(k, 1, 1))
        pright = jnp.where(lane8 == 511, pr_, pltpu.roll(p, 511, 1))
        kright = jnp.where(lane8 == 511, kr_, pltpu.roll(k, 511, 1))
        total = COMPRESS * (p - prev[rows, :])
        total = total + edge_term(p, k, pd, kd) + edge_term(p, k, pu, ku)
        total = total + edge_term(p, k, pright, kright) + edge_term(p, k, pleft, kleft)
        flow_o[rows, :] = total

    mortar_sum = [jnp.zeros((8, 128), F32) for c in range(3)]
    for i in range(NZ - 1, -1, -1):
        if i < NZ - 1:
            remote(xsend.at[i], xrecv.at[i], xss.at[i], xrs.at[i], row(lax.rem(z + FAR[i], NZ))).wait_recv()
        got = (xsend[i] if i == NZ - 1 else xrecv[i]).astype(I32).astype(F32)
        scale = jnp.exp2(got[24:32] - 15.0)
        mortar_sum = [mortar_sum[c] + got[8 * c : 8 * (c + 1)] * scale for c in range(3)]
    jump = [uplus_r[c] - mortar_sum[c] for c in range(3)]
    normal_part = PENALTY * jump[0]
    stress = CONFINING - node_p[...] - normal_part
    softplus = jnp.maximum(stress, 0.0) + jnp.log1p(jnp.exp(-jnp.abs(stress)))
    factor = FRICTION * softplus / jnp.sqrt(jump[1] * jump[1] + jump[2] * jump[2] + 1.0)
    state = state_r[...]
    sliding = [normal_part, jump[1] * factor, jump[2] * factor]
    traction = [
        jnp.where(state == 0, PENALTY * jump[c], jnp.where(state == 1, sliding[c], 0.0)) for c in range(3)
    ]
    tsend[...] = jnp.concatenate(traction + [jnp.zeros((8, 128), F32)], axis=0).astype(BF16)
    tcopies = []
    for i in range(NZ - 1):
        there, back = row(lax.rem(z + FAR[i], NZ)), FAR.index((NZ - FAR[i]) % NZ)
        tcopies.append(remote(tsend, trecv.at[back], tss.at[i], trs.at[back], there))
        tcopies[-1].start()
    trecv[NZ - 1] = tsend[...]
    for c in range(3):
        faces_o[c] = traction[c]

    rcopies = []
    for h in (1, 0):
        for i in range(min(4 * h + 3, NZ - 2), 4 * h - 1, -1):
            remote(tsend, trecv.at[i], tss.at[i], trs.at[i], row(lax.rem(z + FAR[i], NZ))).wait_recv()
        got = trecv[4 * h : 4 * (h + 1)].astype(F32)
        table = jnp.concatenate([got[:, 8 * c : 8 * (c + 1), :].reshape(32, 128) for c in range(3)], axis=1)
        rsend[h] = dot_tn(owner[h], table.astype(BF16)).astype(BF16).reshape(NP, 16, 384)
        for i in COLUMN_ORDER:
            p = lax.rem(pos + i, NP)
            rcopies.append(remote(rsend.at[h, p], rrecv.at[h, pos], rss.at[h, i], rrs.at[h, pos], column(p)))
            rcopies[-1].start()
        rrecv[h, pos] = rsend[h, pos]
    for copy in ccopies + zcopies + hcopies + xcopies + tcopies + rcopies:
        copy.wait_send()
    replies = jnp.zeros((64, 384), F32)
    for h in (1, 0):
        for i in COLUMN_ORDER:
            p = lax.rem(pos + i, NP)
            remote(rsend.at[h, p], rrecv.at[h, p], rss.at[h, i], rrs.at[h, p], column(p)).wait_recv()
        replies = replies + dot_nn(slots_t[:, HALF * h : HALF * (h + 1)], rrecv[h].reshape(HALF, 384))

    patch = iota((8, 128), 0)
    total = jnp.zeros((32, 128), F32)
    for q in range(0, 64, 2):
        left = []
        for k in range(2):
            mine = patch == source_s[q + k]
            rows = [
                jnp.where(mine, jnp.broadcast_to(replies[q + k : q + k + 1, 128 * c : 128 * (c + 1)], (8, 128)), 0.0)
                for c in range(3)
            ]
            left.append(jnp.concatenate(rows + [jnp.zeros((8, 128), F32)], axis=0).astype(BF16))
        total = total + dot_nn(jnp.concatenate(left, axis=1), mort[q : q + 2].reshape(256, 128))
    for c in range(3):
        faces_o[3 + c] = -total[8 * c : 8 * (c + 1), :]


def store_kernel(faces, flow, flow_o, traction_o, force_o, osem):
    stores = [
        pltpu.make_async_copy(faces.at[pl.ds(0, 3)], traction_o, osem.at[0]),
        pltpu.make_async_copy(faces.at[pl.ds(3, 3)], force_o, osem.at[1]),
        pltpu.make_async_copy(flow, flow_o, osem.at[2]),
    ]
    for copy in stores:
        copy.start()
    for copy in stores:
        copy.wait()


def on_device(
    pressure, pressure_prev, permeability, u_plus, u_minus, node_state, node_cell,
    pair_source, pair_dest, pair_target, mortar,
):
    hbm, vmem = (pl.BlockSpec(memory_space=s) for s in (pltpu.HBM, pltpu.VMEM))
    dma = pltpu.SemaphoreType.DMA
    shape = jax.ShapeDtypeStruct
    faces, flow = pl.pallas_call(
        exchange_kernel,
        out_shape=(shape((6, 8, 128), F32), shape((128, 512), F32)),
        in_specs=[hbm] * 11,
        out_specs=(vmem, vmem),
        scratch_shapes=[
            pltpu.VMEM((128, 512), F32),
            pltpu.VMEM((128, 512), F32),
            pltpu.VMEM((128, 512), F32),
            pltpu.VMEM((64, 128, 128), BF16),
            pltpu.VMEM((64, 384), F32),
            pltpu.VMEM((64, 256), BF16),
            pltpu.VMEM((2, 32, HALF), BF16),
            pltpu.VMEM((2, NP, 16, 384), I16),
            pltpu.VMEM((2, NP, 16, 384), I16),
            pltpu.VMEM((NP, 8, 128), F32),
            pltpu.VMEM((NP, 8, 128), F32),
            pltpu.VMEM((NZ, 32, 128), I16),
            pltpu.VMEM((NZ, 32, 128), I16),
            pltpu.VMEM((32, 128), BF16),
            pltpu.VMEM((NZ, 32, 128), BF16),
            pltpu.VMEM((2, NP, 16, 384), BF16),
            pltpu.VMEM((2, NP, 16, 384), BF16),
            pltpu.VMEM((2, 8, 128), F32),
            pltpu.VMEM((2, 8, 128), F32),
            pltpu.VMEM((2, 8, 128), F32),
            pltpu.VMEM((2, 8, 128), F32),
            pltpu.VMEM((8, 128), F32),
            pltpu.VMEM((3, 8, 128), F32),
            pltpu.VMEM((3, 8, 128), BF16),
            pltpu.VMEM((8, 128), I32),
            pltpu.VMEM((8, 128), I32),
            pltpu.VMEM((64,), I32),
            pltpu.VMEM((64,), I32),
            pltpu.SMEM((64,), I32),
            pltpu.VMEM((2, 8, 8, 128), F32),
            dma((4,)), dma((8,)), dma((6,)),
            dma((2, 8)), dma((2, 8)), dma((8,)), dma((8,)), dma((8,)), dma((8,)),
            dma((8,)), dma((8,)), dma((2, 8)), dma((2, 8)), dma((4,)), dma((4,)),
        ],
        compiler_params=pltpu.CompilerParams(
            collective_id=0, has_side_effects=True, vmem_limit_bytes=48 * 1024 * 1024
        ),
        name="exchange",
    )(
        *(
            pltpu.with_memory_space_constraint(a, pltpu.HBM)
            for a in (
                pressure, pressure_prev, permeability, u_plus.transpose(1, 0, 2), u_minus.transpose(1, 0, 2),
                node_state, node_cell, pair_dest.reshape(64), pair_target, pair_source, mortar,
            )
        )
    )
    flow, traction, force = pl.pallas_call(
        store_kernel,
        out_shape=(shape((128, 512), F32), shape((3, 8, 128), F32), shape((3, 8, 128), F32)),
        in_specs=[vmem, vmem],
        out_specs=(hbm, hbm, hbm),
        scratch_shapes=[dma((3,))],
        compiler_params=pltpu.CompilerParams(vmem_limit_bytes=48 * 1024 * 1024),
        name="store",
    )(faces, flow)
    return flow, traction.transpose(1, 0, 2), force.transpose(1, 0, 2)


def solution(mesh):
    both = ("seg", "dev")
    cells, patches = P("seg", "dev"), P(both, None, None)
    placed = (
        cells, cells, cells, patches, patches, P(both, None), P(both, None), P(both), P(both, None), P(both), patches,
    )
    return jax.shard_map(
        on_device, mesh=mesh, in_specs=placed, out_specs=(cells, patches, patches), check_vma=False
    )
```
